256 devices in a mesh: dp: 8 (over z), heads: 4 (over x_hi, core), ctx: 8 (over x_lo, y).
Axes of the slice: x: 4 (x_hi: 2, x_lo: 2; x = x_hi * 2 + x_lo), y: 4, z: 8, core: 2. Of those that a mesh axis runs over, the one named last changes fastest.
Arguments:
- inputs: bfloat16 [8, 2048, 5120], P('dp', 'ctx'), may hold values from -6 to 6
- queries: bfloat16 [8, 2048, 4096], P('dp', 'ctx', 'heads'), may hold values from -6 to 6
- keys: bfloat16 [8, 2048, 512], P('dp', 'ctx', 'heads'), may hold values from -6 to 6
- values: bfloat16 [8, 2048, 512], P('dp', 'ctx', 'heads'), may hold values from -6 to 6
- outputs: bfloat16 [8, 2048, 4096], P('dp', 'ctx', 'heads'), may hold values from -6 to 6
- out_grad: bfloat16 [8, 2048, 4096], P('dp', 'ctx', 'heads'), may hold values from -6 to 6
- lse: float32 [8, 2048, 32], P('dp', 'ctx', 'heads'), may hold values from 6 to 9
- positions: int32 [8, 2048], P('dp', 'ctx'), may hold values from 0 to 2047, as said below
Outputs:
- query_grad: float32 [8, 2048, 4096], P('dp', 'ctx', 'heads')
- key_grad: float32 [8, 2048, 512], P('dp', 'ctx', 'heads')
- value_grad: float32 [8, 2048, 512], P('dp', 'ctx', 'heads')
- weight_grad: float32 [5120, 1024], P(('dp', 'ctx'), 'heads')
The draws below stay inside these ranges and needn't reach their ends.
Inputs may be any that keep to these rules, and one draw needn't show every extreme that they name: Each sequence's positions are a permutation of 0 to 2047 made of 16 runs of 128 rising consecutive positions; each run fills an aligned block of 128 slots and starts at a multiple of 128.
All inputs are finite; a program needn't handle non-finite values.
Results may differ from the reference program's by a relative error of at most 0.0045.
Values may be sent and summed in bfloat16 or wider, within the bound.
No kernel may reach another device: no remote copies, remote signals or barrier semaphores. Data moves between devices by JAX's collectives and lax.ppermute only.
A program may use at most 64 MiB of HBM per device.

```python
import jax
import jax.numpy as jnp
from jax import lax

D = 5120
HD = 128
GROUP = 8
KV_HEADS = 4
TOK_DEV = 256
L = 2048
SEQS = 8
Q_HEADS = 32


def draw_positions(key, part):
    key = jax.random.fold_in(key, 5)
    half = TOK_DEV // 2
    count = L // half
    seq_keys = jax.random.split(key, SEQS)
    order = jax.vmap(lambda one_key: jax.random.permutation(one_key, count))(seq_keys)
    places = order[:, :, None] * half + jnp.arange(half, dtype=jnp.int32)[None, None, :]
    return places.reshape(SEQS, L).astype(jnp.int32)


def spiked(entries, stream_key, source, target, blocks, factor):
    def block_of(dim):
        return (jnp.arange(entries.shape[dim]) // (entries.shape[dim] // blocks)).reshape((-1,) + (1,) * (entries.ndim - 1 - dim))

    first = jax.random.permutation(stream_key, blocks)[block_of(target)]
    far = (block_of(target) + blocks // 2) % blocks
    return jnp.where((block_of(source) == first) | (block_of(source) == far), factor * entries, entries)


def steps_of(rng, shape, shards, low, largest):
    gain = 1.0
    for dim, blocks in shards:
        draws = jax.random.uniform(jax.random.fold_in(jax.random.fold_in(rng, 6), dim), (blocks,), jnp.float32, low / len(shards), largest / len(shards))
        gain = gain * jnp.repeat(jnp.exp(draws), shape[dim] // blocks).reshape((-1,) + (1,) * (len(shape) - 1 - dim))
    return gain


def centred(key, extent, scale, reach, cuts=(), kind=jnp.bfloat16):
    entries = scale * jax.random.normal(key, extent, jnp.float32)
    if cuts:
        entries = entries * steps_of(key, extent, cuts, -0.22, 0.18)
    return jnp.clip(entries, -reach, reach).astype(kind)


def bell_draw_with(key, shape, deviation, limit, cuts, heavy, kind=jnp.bfloat16):
    drawn = deviation * jax.random.normal(key, shape, jnp.float32)
    if cuts:
        drawn = drawn * steps_of(key, shape, cuts, -0.22, 0.18)
    return jnp.clip(spiked(drawn, jax.random.fold_in(key, 3), *heavy), -limit, limit).astype(kind)


def setup_inputs(seed: int = 0) -> dict:
    splits = jax.random.split(jax.random.key(seed), 9)
    return {
        "inputs": bell_draw_with(splits[0], (SEQS, L, D), 1.0, 6.0, ((0, 8), (1, 8)), (1, 2, 8, 2.0)),
        "queries": centred(splits[1], (SEQS, L, Q_HEADS * HD), 1.0, 6.0, ((0, 8), (1, 8), (2, 4))),
        "keys": centred(splits[2], (SEQS, L, KV_HEADS * HD), 1.0, 6.0, ((0, 8), (1, 8), (2, 4))),
        "values": centred(splits[3], (SEQS, L, KV_HEADS * HD), 1.0, 6.0, ((0, 8), (1, 8), (2, 4))),
        "outputs": centred(splits[4], (SEQS, L, Q_HEADS * HD), 1.0, 6.0, ((0, 8), (1, 8), (2, 4))),
        "out_grad": centred(splits[5], (SEQS, L, Q_HEADS * HD), 1.0, 6.0, ((0, 8), (1, 8), (2, 4))),
        "lse": jnp.clip(6.0 + 3.0 * jax.random.uniform(splits[6], (SEQS, L, Q_HEADS), jnp.float32) ** steps_of(splits[6], (SEQS, L, Q_HEADS), ((0, 8), (1, 8), (2, 4)), -0.2, 0.2), 6.0, 9.0),
        "positions": draw_positions(jax.random.fold_in(splits[8], 71), 0),
    }


def group_grads(query_g, key_g, value_g, grad_g, out_g, lse_g, visible):
    factor = HD ** -0.5
    query_f = query_g.reshape(L, GROUP, HD).astype(jnp.float32)
    grad_f = grad_g.reshape(L, GROUP, HD).astype(jnp.float32)
    out_f = out_g.reshape(L, GROUP, HD).astype(jnp.float32)
    key_f = key_g.astype(jnp.float32)
    value_f = value_g.astype(jnp.float32)
    delta = jnp.sum(grad_f * out_f, axis=2)
    scores = jnp.einsum("qgd,kd->gqk", query_f, key_f) * factor
    probs = jnp.where(visible[None], jnp.exp(scores - jnp.transpose(lse_g)[:, :, None]), jnp.float32(0.0))
    dprobs = jnp.einsum("qgd,kd->gqk", grad_f, value_f)
    dscores = probs * (dprobs - jnp.transpose(delta)[:, :, None])
    probs_low = lax.optimization_barrier(probs.astype(jnp.bfloat16)).astype(jnp.float32)
    dscores_low = lax.optimization_barrier(dscores.astype(jnp.bfloat16)).astype(jnp.float32)
    value_part = jnp.einsum("gqk,qgd->kd", probs_low, grad_f)
    key_part = jnp.einsum("gqk,qgd->kd", dscores_low, query_f) * factor
    query_part = (jnp.einsum("gqk,kd->qgd", dscores_low, key_f) * factor).reshape(L, GROUP * HD)
    return query_part, key_part, value_part


def one_sequence(packed):
    inputs_s, queries_s, keys_s, values_s, outputs_s, grad_s, lse_s, positions_s = packed
    visible = positions_s[None, :] <= positions_s[:, None]
    width = GROUP * HD
    query_list, key_list, value_list, both_list = [], [], [], []
    for head in range(KV_HEADS):
        query_part, key_part, value_part = group_grads(
            queries_s[:, head * width:(head + 1) * width],
            keys_s[:, head * HD:(head + 1) * HD],
            values_s[:, head * HD:(head + 1) * HD],
            grad_s[:, head * width:(head + 1) * width],
            outputs_s[:, head * width:(head + 1) * width],
            lse_s[:, head * GROUP:(head + 1) * GROUP],
            visible)
        query_list.append(query_part)
        key_list.append(key_part)
        value_list.append(value_part)
        both_list.append(key_part)
        both_list.append(value_part)
    kv_low = jnp.concatenate(both_list, axis=1).astype(jnp.bfloat16)
    weight = jnp.dot(jnp.transpose(inputs_s), kv_low, preferred_element_type=jnp.float32)
    return (jnp.concatenate(query_list, axis=1), jnp.concatenate(key_list, axis=1),
            jnp.concatenate(value_list, axis=1), weight)


def reference(inputs, queries, keys, values, outputs, out_grad, lse, positions):
    query_grad, key_grad, value_grad, weights = lax.map(
        one_sequence, (inputs, queries, keys, values, outputs, out_grad, lse, positions))
    return query_grad, key_grad, value_grad, jnp.sum(weights, axis=0)
```

```python
import math

import jax
import jax.numpy as jnp
from jax import lax
from jax.experimental import pallas as pl
from jax.experimental.pallas import tpu as pltpu
from jax.sharding import PartitionSpec as P

HD = 128
RUN = 128
PAD = 16
FACTOR = HD ** (-0.5)
LOG2E = math.log2(math.e)
BF16 = jnp.bfloat16
F32 = jnp.float32

ROWS_ROWS = (((1,), (1,)), ((), ()))
COLS_ROWS = (((1,), (0,)), ((), ()))
COLS_COLS = (((0,), (0,)), ((), ()))


def dot(a, b, dims):
    return lax.dot_general(a, b, dims, preferred_element_type=F32)


def attention_kernel(
    query_ref, grad_ref, out_ref, lse_ref, pos_ref, kv_ref, dq_ref, dkv_ref, acc, lse_t
):
    head = pl.program_id(0)
    blocks, rows, _ = kv_ref.shape
    keys = rows - PAD
    tokens = query_ref.shape[0]

    @pl.when(head == 0)
    def _():
        acc[...] = jnp.zeros_like(acc)
        lse_t[...] = jnp.transpose(lse_ref[...]) * LOG2E

    query = query_ref[...]
    grad = grad_ref[...]
    delta = jnp.sum(
        jnp.transpose(grad.astype(F32) * out_ref[...].astype(F32)), axis=0, keepdims=True
    )
    lse = lse_t[pl.ds(head, 1), :]
    query_pos = pos_ref[...].astype(F32)
    offsets = lax.broadcasted_iota(jnp.int32, (RUN, tokens), 0).astype(F32)
    dq = jnp.zeros((tokens, HD), F32)
    for block in range(blocks):
        key = kv_ref[block, :keys, :HD]
        value = kv_ref[block, :keys, HD:]
        scores = dot(key, query, ROWS_ROWS)
        probs = jnp.exp2(scores * (FACTOR * LOG2E) - lse)
        visible = []
        for run in range(keys // RUN):
            start = kv_ref[block, keys + run : keys + run + 1, :1].astype(F32) * RUN
            visible.append(offsets <= query_pos - start)
        probs = jnp.where(jnp.concatenate(visible, axis=0), probs, 0.0)
        dprobs = dot(value, grad, ROWS_ROWS)
        dscores = (probs * (dprobs - delta)).astype(BF16)
        probs = probs.astype(BF16)
        acc[block, :, HD:] += dot(probs, grad, COLS_ROWS)
        acc[block, :, :HD] += dot(dscores, query, COLS_ROWS)
        dq += dot(dscores, key, COLS_COLS)
    dq_ref[...] = dq * FACTOR

    @pl.when(head == pl.num_programs(0) - 1)
    def _():
        dkv_ref[:, :, :HD] = (acc[:, :, :HD] * FACTOR).astype(BF16)
        dkv_ref[:, :, HD:] = acc[:, :, HD:].astype(BF16)


def attention(query, grad, out, lse, pos, kv):
    tokens, width = query.shape
    heads = width // HD
    blocks, rows, cols = kv.shape
    keys = rows - PAD
    by_head = pl.BlockSpec((tokens, HD), lambda h: (0, h))

    def whole(*shape):
        return pl.BlockSpec(shape, lambda h: (0,) * len(shape))

    return pl.pallas_call(
        attention_kernel,
        grid=(heads,),
        in_specs=[
            by_head,
            by_head,
            by_head,
            whole(tokens, heads),
            whole(1, tokens),
            whole(blocks, rows, cols),
        ],
        out_specs=[by_head, whole(blocks, keys, cols)],
        out_shape=[
            jax.ShapeDtypeStruct((tokens, width), F32),
            jax.ShapeDtypeStruct((blocks, keys, cols), BF16),
        ],
        scratch_shapes=[pltpu.VMEM((blocks, keys, cols), F32), pltpu.VMEM((heads, tokens), F32)],
        compiler_params=pltpu.CompilerParams(vmem_limit_bytes=40 * 2**20),
        cost_estimate=pl.CostEstimate(
            flops=10 * blocks * keys * tokens * width,
            bytes_accessed=12 * 2**20,
            transcendentals=blocks * keys * tokens * heads,
        ),
    )(query, grad, out, lse, pos, kv)


def spread_kernel(in_ref, out_ref):
    parts, _, rows, tokens = out_ref.shape
    out_ref[...] = jnp.transpose(in_ref[...]).reshape(parts, 1, rows, tokens)


def spread(inputs, outer, inner):
    tokens, width = inputs.shape
    rows = width // (outer * inner)
    return pl.pallas_call(
        spread_kernel,
        grid=(outer,),
        in_specs=[pl.BlockSpec((tokens, inner * rows), lambda i: (0, i))],
        out_specs=pl.BlockSpec((inner, 1, rows, tokens), lambda i: (0, i, 0, 0)),
        out_shape=jax.ShapeDtypeStruct((inner, outer, rows, tokens), inputs.dtype),
        compiler_params=pltpu.CompilerParams(vmem_limit_bytes=40 * 2**20),
    )(inputs)


def exchange(parts, axis):
    return lax.all_to_all(parts, axis, 0, 0, tiled=True)


def to_all(block, axis):
    return exchange(jnp.broadcast_to(block, (lax.axis_size(axis),) + block.shape), axis)


def shards(inputs, queries, keys, values, outputs, out_grad, lse, positions):
    tokens = queries.shape[1]
    ctx = lax.axis_size("ctx")
    dp = lax.axis_size("dp")
    runs = tokens // RUN
    starts = (positions[0, ::RUN] // RUN).astype(BF16)
    starts = jnp.broadcast_to(starts[:, None], (runs, 2 * HD))
    kv = jnp.concatenate(
        [
            jnp.concatenate([keys[0], values[0]], axis=1),
            starts,
            jnp.zeros((PAD - runs, 2 * HD), BF16),
        ]
    )
    kv = to_all(kv, "ctx")
    turned = exchange(spread(inputs[0], dp, ctx), "ctx")
    query_grad, partial = attention(
        queries[0], out_grad[0], outputs[0], lse[0], positions, kv
    )
    both = jnp.sum(exchange(partial, "ctx").astype(F32), axis=0)
    kv_low = to_all(both.astype(BF16), "ctx")
    terms = jnp.einsum("sdrt,stc->drc", turned, kv_low, preferred_element_type=F32)
    weight_grad = jnp.sum(exchange(terms.astype(BF16), "dp").astype(F32), axis=0)
    return (query_grad[None], both[None, :, :HD], both[None, :, HD:], weight_grad)


def solution(mesh):
    return jax.shard_map(
        shards,
        mesh=mesh,
        in_specs=(
            P("dp", "ctx", None),
            P("dp", "ctx", "heads"),
            P("dp", "ctx", "heads"),
            P("dp", "ctx", "heads"),
            P("dp", "ctx", "heads"),
            P("dp", "ctx", "heads"),
            P("dp", "ctx", "heads"),
            P("dp", "ctx"),
        ),
        out_specs=(
            P("dp", "ctx", "heads"),
            P("dp", "ctx", "heads"),
            P("dp", "ctx", "heads"),
            P(("dp", "ctx"), "heads"),
        ),
        check_vma=False,
    )
```

```python
import math

import jax
import jax.numpy as jnp
from jax import lax
from jax.experimental import pallas as pl
from jax.experimental.pallas import tpu as pltpu
from jax.sharding import PartitionSpec as P

HD = 128
RUN = 128
PAD = 16
PAIR = 2
CHUNK = 1024
VMEM = 60 * 2**20
FACTOR = HD ** (-0.5)
LOG2E = math.log2(math.e)
BF16 = jnp.bfloat16
F32 = jnp.float32

ROWS_ROWS = (((1,), (1,)), ((), ()))
COLS_ROWS = (((1,), (0,)), ((), ()))


def dot(a, b, dims):
    return lax.dot_general(a, b, dims, preferred_element_type=F32)


def pack_kernel(key_ref, value_ref, pos_ref, out_ref):
    tokens = key_ref.shape[0]
    out_ref[0, :tokens, :HD] = key_ref[...]
    out_ref[0, :tokens, HD:] = value_ref[...]
    row = lax.broadcasted_iota(jnp.int32, (PAD, 2 * HD), 0)
    number = jnp.zeros((PAD, 2 * HD), F32)
    for run in range(tokens // RUN):
        first = pos_ref[:, run * RUN : run * RUN + 1].astype(F32) * (1.0 / RUN)
        number = jnp.where(row == run, first, number)
    out_ref[0, tokens:, :] = number.astype(BF16)


def packed(keys, values, pos, copies):
    tokens = keys.shape[0]
    return pl.pallas_call(
        pack_kernel,
        grid=(copies,),
        in_specs=[
            pl.BlockSpec((tokens, HD), lambda i: (0, 0)),
            pl.BlockSpec((tokens, HD), lambda i: (0, 0)),
            pl.BlockSpec((1, tokens), lambda i: (0, 0)),
        ],
        out_specs=pl.BlockSpec((1, tokens + PAD, 2 * HD), lambda i: (i, 0, 0)),
        out_shape=jax.ShapeDtypeStruct((copies, tokens + PAD, 2 * HD), BF16),
        compiler_params=pltpu.CompilerParams(vmem_limit_bytes=VMEM),
        name="pack",
    )(keys, values, pos)


def attention_kernel(
    query_ref, grad_ref, out_ref, lse_ref, pos_ref, kv_ref, dq_ref, dkv_ref, key, key_t, value, acc
):
    step = pl.program_id(0)
    blocks, rows, _ = kv_ref.shape
    keys = rows - PAD
    tokens = query_ref.shape[0]

    @pl.when(step == 0)
    def _():
        acc[...] = jnp.zeros_like(acc)
        for block in range(blocks):
            here = slice(block * keys, (block + 1) * keys)
            key[here, :] = kv_ref[block, :keys, :HD]
            value[here, :] = kv_ref[block, :keys, HD:]
            key_t[:, here] = jnp.transpose(kv_ref[block, :keys, :HD])

    query_pos = pos_ref[...].astype(F32)
    offsets = lax.broadcasted_iota(jnp.int32, (RUN, tokens), 0).astype(F32)
    for chunk in range(blocks * keys // CHUNK):
        here = slice(chunk * CHUNK, (chunk + 1) * CHUNK)
        visible = []
        for run in range(chunk * CHUNK // RUN, (chunk + 1) * CHUNK // RUN):
            block, row = run // (keys // RUN), keys + run % (keys // RUN)
            start = kv_ref[block, row : row + 1, :1].astype(F32) * RUN
            visible.append(offsets <= query_pos - start)
        visible = jnp.concatenate(visible, axis=0)
        key_part = None
        value_part = None
        for i in range(PAIR):
            cols = slice(i * HD, (i + 1) * HD)
            query = query_ref[:, cols]
            grad = grad_ref[:, cols]
            delta = jnp.sum(
                jnp.transpose(grad.astype(F32) * out_ref[:, cols].astype(F32)),
                axis=0,
                keepdims=True,
            )
            lse = lse_ref[pl.ds(step * PAIR + i, 1), :] * LOG2E
            scores = dot(key[here, :], query, ROWS_ROWS)
            probs = jnp.where(visible, jnp.exp2(scores * (FACTOR * LOG2E) - lse), 0.0)
            dprobs = dot(value[here, :], grad, ROWS_ROWS)
            dscores = (probs * (dprobs - delta)).astype(BF16)
            dv = dot(probs.astype(BF16), grad, COLS_ROWS)
            dk = dot(dscores, query, COLS_ROWS)
            dq = jnp.transpose(dot(key_t[:, here], dscores, COLS_ROWS)) * FACTOR
            if chunk == 0:
                dq_ref[:, cols] = dq
            else:
                dq_ref[:, cols] += dq
            key_part = dk if key_part is None else key_part + dk
            value_part = dv if value_part is None else value_part + dv
        acc[here, :HD] += key_part
        acc[here, HD:] += value_part

    @pl.when(step == pl.num_programs(0) - 1)
    def _():
        for block in range(blocks):
            here = slice(block * keys, (block + 1) * keys)
            dkv_ref[block, :, :HD] = (acc[here, :HD] * FACTOR).astype(BF16)
            dkv_ref[block, :, HD:] = acc[here, HD:].astype(BF16)


def attention(query, grad, out, lse, pos, kv):
    tokens, width = query.shape
    heads = width // HD
    blocks, rows, cols = kv.shape
    keys = rows - PAD
    by_head = pl.BlockSpec((tokens, PAIR * HD), lambda h: (0, h))

    def whole(*shape):
        return pl.BlockSpec(shape, lambda h: (0,) * len(shape))

    return pl.pallas_call(
        attention_kernel,
        grid=(heads // PAIR,),
        in_specs=[
            by_head,
            by_head,
            by_head,
            whole(heads, tokens),
            whole(1, tokens),
            whole(blocks, rows, cols),
        ],
        out_specs=[by_head, whole(blocks, keys, cols)],
        out_shape=[
            jax.ShapeDtypeStruct((tokens, width), F32),
            jax.ShapeDtypeStruct((blocks, keys, cols), BF16),
        ],
        scratch_shapes=[
            pltpu.VMEM((blocks * keys, HD), BF16),
            pltpu.VMEM((HD, blocks * keys), BF16),
            pltpu.VMEM((blocks * keys, HD), BF16),
            pltpu.VMEM((blocks * keys, cols), F32),
        ],
        compiler_params=pltpu.CompilerParams(vmem_limit_bytes=VMEM),
        cost_estimate=pl.CostEstimate(
            flops=10 * blocks * keys * tokens * width,
            bytes_accessed=12 * 2**20,
            transcendentals=blocks * keys * tokens * heads,
        ),
        name="attention",
    )(query, grad, out, lse, pos, kv)


def spread_kernel(half_ref, in_ref, out_ref):
    parts, _, rows, tokens = out_ref.shape
    out_ref[...] = jnp.transpose(in_ref[...]).reshape(parts, 1, rows, tokens)


def spread(inputs, half, outer, inner):
    tokens, width = inputs.shape
    tokens = tokens // 2
    rows = width // (outer * inner)
    return pl.pallas_call(
        spread_kernel,
        grid_spec=pltpu.PrefetchScalarGridSpec(
            num_scalar_prefetch=1,
            grid=(outer,),
            in_specs=[pl.BlockSpec((tokens, inner * rows), lambda i, h: (h[0], i))],
            out_specs=pl.BlockSpec((inner, 1, rows, tokens), lambda i, h: (0, i, 0, 0)),
        ),
        out_shape=jax.ShapeDtypeStruct((inner, outer, rows, tokens), inputs.dtype),
        compiler_params=pltpu.CompilerParams(vmem_limit_bytes=VMEM),
        name="spread",
    )(half, inputs)


def project_kernel(own_ref, other_ref, kv_ref, out_ref):
    blocks, _, tokens = own_ref.shape
    total = None
    for block in range(blocks):
        for half, ref in enumerate((own_ref, other_ref)):
            here = slice(half * tokens, (half + 1) * tokens)
            term = dot(ref[block], kv_ref[block, here, :], COLS_ROWS)
            total = term if total is None else total + term
    out_ref[...] = total.astype(BF16)


def project(own, other, kv):
    rows = own.shape[1]
    cols = kv.shape[2]
    return pl.pallas_call(
        project_kernel,
        out_shape=jax.ShapeDtypeStruct((rows, cols), BF16),
        compiler_params=pltpu.CompilerParams(vmem_limit_bytes=32 * 2**20),
        name="project",
    )(own, other, kv)


def exchange(parts, axis):
    return lax.all_to_all(parts, axis, 0, 0, tiled=True)


def with_neighbour(block):
    devices = range(lax.axis_size("heads"))
    return lax.ppermute(block, "heads", [(i, i ^ 1) for i in devices])


def shards(inputs, queries, keys, values, outputs, out_grad, lse, positions):
    tokens = queries.shape[1]
    ctx = lax.axis_size("ctx")
    dp = lax.axis_size("dp")
    half = lax.axis_index("heads") % 2
    kv = exchange(packed(keys[0], values[0], positions, ctx), "ctx")
    turned = spread(inputs[0], half.reshape(1), dp, ctx)
    kv, turned = lax.optimization_barrier((kv, turned))
    own = exchange(turned, "ctx")
    query_grad, partial = attention(
        queries[0], out_grad[0], outputs[0], jnp.transpose(lse[0]), positions, kv
    )
    partial, own = lax.optimization_barrier((partial, own))
    own = own.reshape(ctx, -1, tokens // 2)
    other = with_neighbour(own)
    both = jnp.sum(exchange(partial, "ctx").astype(F32), axis=0)
    kv_low = both.astype(BF16)
    kv_low = jnp.where(half == 0, kv_low, jnp.roll(kv_low, tokens // 2, axis=0))
    kv_low = exchange(jnp.broadcast_to(kv_low, (ctx,) + kv_low.shape), "ctx")
    terms = project(own, other, kv_low).reshape(dp, -1, 2 * HD)
    weight_grad = jnp.sum(exchange(terms, "dp").astype(F32), axis=0)
    return (query_grad[None], both[None, :, :HD], both[None, :, HD:], weight_grad)


def solution(mesh):
    return jax.shard_map(
        shards,
        mesh=mesh,
        in_specs=(
            P("dp", "ctx", None),
            P("dp", "ctx", "heads"),
            P("dp", "ctx", "heads"),
            P("dp", "ctx", "heads"),
            P("dp", "ctx", "heads"),
            P("dp", "ctx", "heads"),
            P("dp", "ctx", "heads"),
            P("dp", "ctx"),
        ),
        out_specs=(
            P("dp", "ctx", "heads"),
            P("dp", "ctx", "heads"),
            P("dp", "ctx", "heads"),
            P(("dp", "ctx"), "heads"),
        ),
        check_vma=False,
    )
```

```python
import functools
import math

import jax
import jax.numpy as jnp
from jax import lax
from jax.experimental import pallas as pl
from jax.experimental.pallas import tpu as pltpu
from jax.sharding import PartitionSpec as P

HD = 128
RUN = 128
PAD = 16
PAIR = 2
CHUNK = 1024
VMEM = 60 * 2**20
FACTOR = HD ** (-0.5)
LOG2E = math.log2(math.e)
BF16 = jnp.bfloat16
F32 = jnp.float32

ROWS_ROWS = (((1,), (1,)), ((), ()))
COLS_ROWS = (((1,), (0,)), ((), ()))


def dot(a, b, dims):
    return lax.dot_general(a, b, dims, preferred_element_type=F32)


def pack_kernel(key_ref, value_ref, pos_ref, out_ref, block, sems):
    tokens = key_ref.shape[0]
    block[:tokens, :HD] = key_ref[...]
    block[:tokens, HD:] = value_ref[...]
    row = lax.broadcasted_iota(jnp.int32, (PAD, 2 * HD), 0)
    number = jnp.zeros((PAD, 2 * HD), F32)
    for run in range(tokens // RUN):
        first = pos_ref[:, run * RUN : run * RUN + 1].astype(F32) * (1.0 / RUN)
        number = jnp.where(row == run, first, number)
    block[tokens:, :] = number.astype(BF16)
    copies = [
        pltpu.make_async_copy(block, out_ref.at[i], sems.at[i]) for i in range(out_ref.shape[0])
    ]
    for copy in copies:
        copy.start()
    for copy in copies:
        copy.wait()


def packed(keys, values, pos, copies):
    rows = keys.shape[0] + PAD
    return pl.pallas_call(
        pack_kernel,
        out_specs=pl.BlockSpec(memory_space=pl.ANY),
        out_shape=jax.ShapeDtypeStruct((copies, rows, 2 * HD), BF16),
        scratch_shapes=[pltpu.VMEM((rows, 2 * HD), BF16), pltpu.SemaphoreType.DMA((copies,))],
        compiler_params=pltpu.CompilerParams(vmem_limit_bytes=VMEM),
        name="pack",
    )(keys, values, pos)


def attention_kernel(
    query_ref, grad_ref, out_ref, lse_ref, pos_ref, kv_ref, dq_ref, dkv_ref, key, key_t, value, acc
):
    step = pl.program_id(0)
    blocks, rows, _ = kv_ref.shape
    keys = rows - PAD
    tokens = query_ref.shape[0]

    @pl.when(step == 0)
    def _():
        acc[...] = jnp.zeros_like(acc)
        for block in range(blocks):
            here = slice(block * keys, (block + 1) * keys)
            key[here, :] = kv_ref[block, :keys, :HD]
            value[here, :] = kv_ref[block, :keys, HD:]
            key_t[:, here] = jnp.transpose(kv_ref[block, :keys, :HD])

    query_pos = pos_ref[...].astype(F32)
    offsets = lax.broadcasted_iota(jnp.int32, (RUN, tokens), 0).astype(F32)
    for chunk in range(blocks * keys // CHUNK):
        here = slice(chunk * CHUNK, (chunk + 1) * CHUNK)
        visible = []
        for run in range(chunk * CHUNK // RUN, (chunk + 1) * CHUNK // RUN):
            block, row = run // (keys // RUN), keys + run % (keys // RUN)
            start = kv_ref[block, row : row + 1, :1].astype(F32) * RUN
            visible.append(offsets <= query_pos - start)
        visible = jnp.concatenate(visible, axis=0)
        key_part = None
        value_part = None
        for i in range(PAIR):
            cols = slice(i * HD, (i + 1) * HD)
            query = query_ref[:, cols]
            grad = grad_ref[:, cols]
            delta = jnp.sum(
                jnp.transpose(grad.astype(F32) * out_ref[:, cols].astype(F32)),
                axis=0,
                keepdims=True,
            )
            lse = lse_ref[pl.ds(step * PAIR + i, 1), :] * LOG2E
            scores = dot(key[here, :], query, ROWS_ROWS)
            probs = jnp.where(visible, jnp.exp2(scores * (FACTOR * LOG2E) - lse), 0.0)
            dprobs = dot(value[here, :], grad, ROWS_ROWS)
            dscores = (probs * (dprobs - delta)).astype(BF16)
            dv = dot(probs.astype(BF16), grad, COLS_ROWS)
            dk = dot(dscores, query, COLS_ROWS)
            dq = jnp.transpose(dot(key_t[:, here], dscores, COLS_ROWS)) * FACTOR
            if chunk == 0:
                dq_ref[:, cols] = dq
            else:
                dq_ref[:, cols] += dq
            key_part = dk if key_part is None else key_part + dk
            value_part = dv if value_part is None else value_part + dv
        acc[here, :HD] += key_part
        acc[here, HD:] += value_part

    @pl.when(step == pl.num_programs(0) - 1)
    def _():
        for block in range(blocks):
            here = slice(block * keys, (block + 1) * keys)
            dkv_ref[block, :, :HD] = (acc[here, :HD] * FACTOR).astype(BF16)
            dkv_ref[block, :, HD:] = acc[here, HD:].astype(BF16)


def attention(query, grad, out, lse, pos, kv):
    tokens, width = query.shape
    heads = width // HD
    blocks, rows, cols = kv.shape
    keys = rows - PAD
    by_head = pl.BlockSpec((tokens, PAIR * HD), lambda h: (0, h))

    def whole(*shape):
        return pl.BlockSpec(shape, lambda h: (0,) * len(shape))

    return pl.pallas_call(
        attention_kernel,
        grid=(heads // PAIR,),
        in_specs=[
            by_head,
            by_head,
            by_head,
            whole(heads, tokens),
            whole(1, tokens),
            whole(blocks, rows, cols),
        ],
        out_specs=[by_head, whole(blocks, keys, cols)],
        out_shape=[
            jax.ShapeDtypeStruct((tokens, width), F32),
            jax.ShapeDtypeStruct((blocks, keys, cols), BF16),
        ],
        scratch_shapes=[
            pltpu.VMEM((blocks * keys, HD), BF16),
            pltpu.VMEM((HD, blocks * keys), BF16),
            pltpu.VMEM((blocks * keys, HD), BF16),
            pltpu.VMEM((blocks * keys, cols), F32),
        ],
        compiler_params=pltpu.CompilerParams(vmem_limit_bytes=VMEM),
        cost_estimate=pl.CostEstimate(
            flops=10 * blocks * keys * tokens * width,
            bytes_accessed=12 * 2**20,
            transcendentals=blocks * keys * tokens * heads,
        ),
        name="attention",
    )(query, grad, out, lse, pos, kv)


def spread_kernel(half, outer, inner, turn_ref, in_ref, *refs):
    out_ref, block, turned, in_sems, out_sems = refs[-5:]
    tokens = block.shape[1]
    width = block.shape[2]

    @pl.when(turn_ref[0] == half)
    def _():
        here = pl.ds(pl.multiple_of(turn_ref[1] * tokens, tokens), tokens)
        loads = [
            pltpu.make_async_copy(
                in_ref.at[here, pl.ds(i * width, width)], block.at[i], in_sems.at[i]
            )
            for i in range(outer)
        ]
        stores = [
            pltpu.make_async_copy(turned.at[:, i], out_ref.at[:, i], out_sems.at[i])
            for i in range(outer)
        ]
        for load in loads:
            load.start()
        for i in range(outer):
            loads[i].wait()
            turned[:, i] = jnp.transpose(block[i]).reshape(inner, width // inner, tokens)
            stores[i].start()
        for store in stores:
            store.wait()


def spread(inputs, turn, half, outer, inner, before=None):
    tokens, width = inputs.shape
    tokens = tokens // 2
    width = width // outer
    shape = (inner, outer, width // inner, tokens)
    given = () if before is None else (before,)
    anywhere = pl.BlockSpec(memory_space=pl.ANY)
    return pl.pallas_call(
        functools.partial(spread_kernel, half, outer, inner),
        in_specs=[pl.BlockSpec(memory_space=pltpu.SMEM), anywhere] + [anywhere for _ in given],
        out_specs=anywhere,
        out_shape=jax.ShapeDtypeStruct(shape, inputs.dtype),
        input_output_aliases={2: 0} if given else {},
        scratch_shapes=[
            pltpu.VMEM((outer, tokens, width), inputs.dtype),
            pltpu.VMEM(shape, inputs.dtype),
            pltpu.SemaphoreType.DMA((outer,)),
            pltpu.SemaphoreType.DMA((outer,)),
        ],
        compiler_params=pltpu.CompilerParams(vmem_limit_bytes=VMEM),
        name="spread",
    )(turn, inputs, *given)


def exchange(parts, axis):
    return lax.all_to_all(parts, axis, 0, 0, tiled=True)


def with_neighbour(block):
    devices = range(lax.axis_size("heads"))
    return lax.ppermute(block, "heads", [(i, i ^ 1) for i in devices])


def shards(inputs, queries, keys, values, outputs, out_grad, lse, positions):
    tokens = queries.shape[1]
    ctx = lax.axis_size("ctx")
    dp = lax.axis_size("dp")
    half = lax.axis_index("heads") % 2
    turn = jnp.stack([half, half])
    kv = packed(keys[0], values[0], positions, ctx)
    turned = spread(inputs[0], turn, 1, dp, ctx)
    kv, turned = lax.optimization_barrier((kv, turned))
    kv = exchange(kv, "ctx")
    turned = spread(inputs[0], turn, 0, dp, ctx, turned)
    kv, turned = lax.optimization_barrier((kv, turned))
    own = exchange(turned, "ctx")
    query_grad, partial = attention(
        queries[0], out_grad[0], outputs[0], jnp.transpose(lse[0]), positions, kv
    )
    partial, own = lax.optimization_barrier((partial, own))
    own = own.reshape(ctx, -1, tokens // 2)
    other = with_neighbour(own)
    both = jnp.sum(exchange(partial, "ctx").astype(F32), axis=0)
    kv_low = jnp.broadcast_to(both.astype(BF16), (ctx,) + both.shape)
    kv_low = exchange(kv_low, "ctx")
    first = half == 0
    turned = jnp.concatenate(
        [jnp.where(first, own, other), jnp.where(first, other, own)], axis=2
    )
    kv_low, turned = lax.optimization_barrier((kv_low, turned))
    terms = jnp.einsum("srt,stc->rc", turned, kv_low, preferred_element_type=F32)
    terms = terms.astype(BF16).reshape(dp, -1, 2 * HD)
    weight_grad = jnp.sum(exchange(terms, "dp").astype(F32), axis=0)
    return (query_grad[None], both[None, :, :HD], both[None, :, HD:], weight_grad)


def solution(mesh):
    return jax.shard_map(
        shards,
        mesh=mesh,
        in_specs=(
            P("dp", "ctx", None),
            P("dp", "ctx", "heads"),
            P("dp", "ctx", "heads"),
            P("dp", "ctx", "heads"),
            P("dp", "ctx", "heads"),
            P("dp", "ctx", "heads"),
            P("dp", "ctx", "heads"),
            P("dp", "ctx"),
        ),
        out_specs=(
            P("dp", "ctx", "heads"),
            P("dp", "ctx", "heads"),
            P("dp", "ctx", "heads"),
            P(("dp", "ctx"), "heads"),
        ),
        check_vma=False,
    )
```

```python
import functools
import math

import jax
import jax.numpy as jnp
from jax import lax
from jax.experimental import pallas as pl
from jax.experimental.pallas import tpu as pltpu
from jax.sharding import PartitionSpec as P

HD = 128
RUN = 128
PAD = 16
PAIR = 2
CHUNK = 1024
VMEM = 60 * 2**20
CTX_ORDER = (0, 6)
DP_ORDER = (2, 6)
FACTOR = HD ** (-0.5)
LOG2E = math.log2(math.e)
BF16 = jnp.bfloat16
F32 = jnp.float32

ROWS_ROWS = (((1,), (1,)), ((), ()))
COLS_ROWS = (((1,), (0,)), ((), ()))


def dot(a, b, dims):
    return lax.dot_general(a, b, dims, preferred_element_type=F32)


def pack_kernel(key_ref, value_ref, pos_ref, out_ref, block, sems):
    tokens = key_ref.shape[0]
    block[:tokens, :HD] = key_ref[...]
    block[:tokens, HD:] = value_ref[...]
    row = lax.broadcasted_iota(jnp.int32, (PAD, 2 * HD), 0)
    number = jnp.zeros((PAD, 2 * HD), F32)
    for run in range(tokens // RUN):
        first = pos_ref[:, run * RUN : run * RUN + 1].astype(F32) * (1.0 / RUN)
        number = jnp.where(row == run, first, number)
    block[tokens:, :] = number.astype(BF16)
    copies = [
        pltpu.make_async_copy(block, out_ref.at[i], sems.at[i]) for i in range(out_ref.shape[0])
    ]
    for copy in copies:
        copy.start()
    for copy in copies:
        copy.wait()


def packed(keys, values, pos, copies):
    rows = keys.shape[0] + PAD
    return pl.pallas_call(
        pack_kernel,
        out_specs=pl.BlockSpec(memory_space=pl.ANY),
        out_shape=jax.ShapeDtypeStruct((copies, rows, 2 * HD), BF16),
        scratch_shapes=[pltpu.VMEM((rows, 2 * HD), BF16), pltpu.SemaphoreType.DMA((copies,))],
        compiler_params=pltpu.CompilerParams(vmem_limit_bytes=VMEM),
        name="pack",
    )(keys, values, pos)


def attention_kernel(
    query_ref, grad_ref, out_ref, lse_ref, pos_ref, kv_ref, dq_ref, dkv_ref, key, key_t, value, acc
):
    step = pl.program_id(0)
    blocks, rows, _ = kv_ref.shape
    keys = rows - PAD
    tokens = query_ref.shape[0]

    @pl.when(step == 0)
    def _():
        acc[...] = jnp.zeros_like(acc)
        for block in range(blocks):
            here = slice(block * keys, (block + 1) * keys)
            key[here, :] = kv_ref[block, :keys, :HD]
            value[here, :] = kv_ref[block, :keys, HD:]
            key_t[:, here] = jnp.transpose(kv_ref[block, :keys, :HD])

    query_pos = pos_ref[...].astype(F32)
    offsets = lax.broadcasted_iota(jnp.int32, (RUN, tokens), 0).astype(F32)
    for chunk in range(blocks * keys // CHUNK):
        here = slice(chunk * CHUNK, (chunk + 1) * CHUNK)
        visible = []
        for run in range(chunk * CHUNK // RUN, (chunk + 1) * CHUNK // RUN):
            block, row = run // (keys // RUN), keys + run % (keys // RUN)
            start = kv_ref[block, row : row + 1, :1].astype(F32) * RUN
            visible.append(offsets <= query_pos - start)
        visible = jnp.concatenate(visible, axis=0)
        key_part = None
        value_part = None
        for i in range(PAIR):
            cols = slice(i * HD, (i + 1) * HD)
            query = query_ref[:, cols]
            grad = grad_ref[:, cols]
            delta = jnp.sum(
                jnp.transpose(grad.astype(F32) * out_ref[:, cols].astype(F32)),
                axis=0,
                keepdims=True,
            )
            lse = lse_ref[pl.ds(step * PAIR + i, 1), :] * LOG2E
            scores = dot(key[here, :], query, ROWS_ROWS)
            probs = jnp.where(visible, jnp.exp2(scores * (FACTOR * LOG2E) - lse), 0.0)
            dprobs = dot(value[here, :], grad, ROWS_ROWS)
            dscores = (probs * (dprobs - delta)).astype(BF16)
            dv = dot(probs.astype(BF16), grad, COLS_ROWS)
            dk = dot(dscores, query, COLS_ROWS)
            dq = jnp.transpose(dot(key_t[:, here], dscores, COLS_ROWS)) * FACTOR
            if chunk == 0:
                dq_ref[:, cols] = dq
            else:
                dq_ref[:, cols] += dq
            key_part = dk if key_part is None else key_part + dk
            value_part = dv if value_part is None else value_part + dv
        acc[here, :HD] += key_part
        acc[here, HD:] += value_part

    @pl.when(step == pl.num_programs(0) - 1)
    def _():
        for block in range(blocks):
            here = slice(block * keys, (block + 1) * keys)
            dkv_ref[block, :, :HD] = (acc[here, :HD] * FACTOR).astype(BF16)
            dkv_ref[block, :, HD:] = acc[here, HD:].astype(BF16)


def attention(query, grad, out, lse, pos, kv):
    tokens, width = query.shape
    heads = width // HD
    blocks, rows, cols = kv.shape
    keys = rows - PAD
    by_head = pl.BlockSpec((tokens, PAIR * HD), lambda h: (0, h))

    def whole(*shape):
        return pl.BlockSpec(shape, lambda h: (0,) * len(shape))

    return pl.pallas_call(
        attention_kernel,
        grid=(heads // PAIR,),
        in_specs=[
            by_head,
            by_head,
            by_head,
            whole(heads, tokens),
            whole(1, tokens),
            whole(blocks, rows, cols),
        ],
        out_specs=[by_head, whole(blocks, keys, cols)],
        out_shape=[
            jax.ShapeDtypeStruct((tokens, width), F32),
            jax.ShapeDtypeStruct((blocks, keys, cols), BF16),
        ],
        scratch_shapes=[
            pltpu.VMEM((blocks * keys, HD), BF16),
            pltpu.VMEM((HD, blocks * keys), BF16),
            pltpu.VMEM((blocks * keys, HD), BF16),
            pltpu.VMEM((blocks * keys, cols), F32),
        ],
        compiler_params=pltpu.CompilerParams(vmem_limit_bytes=VMEM),
        cost_estimate=pl.CostEstimate(
            flops=10 * blocks * keys * tokens * width,
            bytes_accessed=12 * 2**20,
            transcendentals=blocks * keys * tokens * heads,
        ),
        name="attention",
    )(query, grad, out, lse, pos, kv)


def spread_kernel(outer, inner, half_ref, in_ref, out_ref, block, turned, in_sems, out_sems):
    half = half_ref[0]
    mask = jnp.where(half == 0, CTX_ORDER[0], CTX_ORDER[1])
    tokens = block.shape[1]
    width = block.shape[2]
    rows = width // inner
    here = pl.ds(pl.multiple_of(half * tokens, tokens), tokens)
    loads = [
        pltpu.make_async_copy(
            in_ref.at[here, pl.ds(i * width, width)], block.at[i], in_sems.at[i]
        )
        for i in range(outer)
    ]
    stores = [
        pltpu.make_async_copy(turned.at[:, i], out_ref.at[:, i], out_sems.at[i])
        for i in range(outer)
    ]
    for load in loads:
        load.start()
    for i in range(outer):
        loads[i].wait()
        columns = jnp.transpose(block[i])
        for piece in range(inner):
            turned[jnp.bitwise_xor(piece, mask), i] = columns[piece * rows : (piece + 1) * rows]
        stores[i].start()
    for store in stores:
        store.wait()


def spread(inputs, half, outer, inner):
    tokens, width = inputs.shape
    tokens = tokens // 2
    width = width // outer
    shape = (inner, outer, width // inner, tokens)
    anywhere = pl.BlockSpec(memory_space=pl.ANY)
    return pl.pallas_call(
        functools.partial(spread_kernel, outer, inner),
        in_specs=[pl.BlockSpec(memory_space=pltpu.SMEM), anywhere],
        out_specs=anywhere,
        out_shape=jax.ShapeDtypeStruct(shape, inputs.dtype),
        scratch_shapes=[
            pltpu.VMEM((outer, tokens, width), inputs.dtype),
            pltpu.VMEM(shape, inputs.dtype),
            pltpu.SemaphoreType.DMA((outer,)),
            pltpu.SemaphoreType.DMA((outer,)),
        ],
        compiler_params=pltpu.CompilerParams(vmem_limit_bytes=VMEM),
        name="spread",
    )(half, inputs)


def join_kernel(half_ref, own_ref, other_ref, out_ref):
    first = half_ref[0] == 0
    mask = jnp.where(first, DP_ORDER[0], DP_ORDER[1])
    tokens = own_ref.shape[3]
    for i in range(out_ref.shape[1]):
        index = jnp.bitwise_xor(i, mask)
        own = own_ref[0, index]
        other = other_ref[0, index]
        out_ref[0, i, :, :tokens] = jnp.where(first, own, other)
        out_ref[0, i, :, tokens:] = jnp.where(first, other, own)


def join(own, other, half):
    inner, outer, rows, tokens = own.shape
    swap = CTX_ORDER[0] ^ CTX_ORDER[1]
    return pl.pallas_call(
        join_kernel,
        grid=(inner,),
        in_specs=[
            pl.BlockSpec(memory_space=pltpu.SMEM),
            pl.BlockSpec((1, outer, rows, tokens), lambda i: (i, 0, 0, 0)),
            pl.BlockSpec((1, outer, rows, tokens), lambda i: (jnp.bitwise_xor(i, swap), 0, 0, 0)),
        ],
        out_specs=pl.BlockSpec((1, outer, rows, 2 * tokens), lambda i: (i, 0, 0, 0)),
        out_shape=jax.ShapeDtypeStruct((inner, outer, rows, 2 * tokens), own.dtype),
        compiler_params=pltpu.CompilerParams(vmem_limit_bytes=16 * 2**20),
        name="join",
    )(half, own, other)


def exchange_ctx(parts):
    heads, ctx = lax.axis_size("heads"), lax.axis_size("ctx")
    groups = [[h * ctx + (i ^ CTX_ORDER[h % 2]) for i in range(ctx)] for h in range(heads)]
    return lax.all_to_all(
        parts, ("heads", "ctx"), 0, 0, axis_index_groups=groups, tiled=True
    )


def exchange_dp(parts):
    heads, dp = lax.axis_size("heads"), lax.axis_size("dp")
    groups = [[(i ^ DP_ORDER[h % 2]) * heads + h for i in range(dp)] for h in range(heads)]
    return lax.all_to_all(parts, ("dp", "heads"), 0, 0, axis_index_groups=groups, tiled=True)


def with_neighbour(block):
    devices = range(lax.axis_size("heads"))
    return lax.ppermute(block, "heads", [(i, i ^ 1) for i in devices])


def shards(inputs, queries, keys, values, outputs, out_grad, lse, positions):
    ctx = lax.axis_size("ctx")
    dp = lax.axis_size("dp")
    half = (lax.axis_index("heads") % 2).reshape(1)
    kv = exchange_ctx(packed(keys[0], values[0], positions, ctx))
    turned = spread(inputs[0], half, dp, ctx)
    kv, turned = lax.optimization_barrier((kv, turned))
    own = exchange_ctx(turned)
    query_grad, partial = attention(
        queries[0], out_grad[0], outputs[0], jnp.transpose(lse[0]), positions, kv
    )
    partial, own = lax.optimization_barrier((partial, own))
    turned = join(own, with_neighbour(own), half)
    partial, turned = lax.optimization_barrier((exchange_ctx(partial), turned))
    both = jnp.sum(partial.astype(F32), axis=0)
    kv_low = jnp.broadcast_to(both.astype(BF16), (ctx,) + both.shape)
    kv_low = exchange_ctx(kv_low)
    turned = turned.reshape(ctx, -1, turned.shape[-1])
    terms = jnp.einsum("srt,stc->rc", turned, kv_low, preferred_element_type=F32)
    terms, both = lax.optimization_barrier((terms.astype(BF16), both))
    terms = exchange_dp(terms.reshape(dp, -1, 2 * HD))
    weight_grad = jnp.sum(terms.astype(F32), axis=0)
    return (query_grad[None], both[None, :, :HD], both[None, :, HD:], weight_grad)


def solution(mesh):
    return jax.shard_map(
        shards,
        mesh=mesh,
        in_specs=(
            P("dp", "ctx", None),
            P("dp", "ctx", "heads"),
            P("dp", "ctx", "heads"),
            P("dp", "ctx", "heads"),
            P("dp", "ctx", "heads"),
            P("dp", "ctx", "heads"),
            P("dp", "ctx", "heads"),
            P("dp", "ctx"),
        ),
        out_specs=(
            P("dp", "ctx", "heads"),
            P("dp", "ctx", "heads"),
            P("dp", "ctx", "heads"),
            P(("dp", "ctx"), "heads"),
        ),
        check_vma=False,
    )
```

```python
import functools
import math

import jax
import jax.numpy as jnp
from jax import lax
from jax.experimental import pallas as pl
from jax.experimental.pallas import tpu as pltpu
from jax.sharding import PartitionSpec as P

HD = 128
RUN = 128
PAD = 16
PAIR = 2
CHUNK = 1024
VMEM = 60 * 2**20
X = 2
Y = 4
CTX_ORDER = (0, 6)
DP_ORDER = (2, 6)
FACTOR = HD ** (-0.5)
LOG2E = math.log2(math.e)
BF16 = jnp.bfloat16
F32 = jnp.float32

ROWS_ROWS = (((1,), (1,)), ((), ()))
COLS_ROWS = (((1,), (0,)), ((), ()))


def dot(a, b, dims):
    return lax.dot_general(a, b, dims, preferred_element_type=F32)


def pack_kernel(key_ref, value_ref, pos_ref, out_ref, block, sems):
    tokens = key_ref.shape[0]
    block[:tokens, :HD] = key_ref[...]
    block[:tokens, HD:] = value_ref[...]
    row = lax.broadcasted_iota(jnp.int32, (PAD, 2 * HD), 0)
    number = jnp.zeros((PAD, 2 * HD), F32)
    for run in range(tokens // RUN):
        first = pos_ref[:, run * RUN : run * RUN + 1].astype(F32) * (1.0 / RUN)
        number = jnp.where(row == run, first, number)
    block[tokens:, :] = number.astype(BF16)
    copies = [
        pltpu.make_async_copy(block, out_ref.at[i], sems.at[i]) for i in range(out_ref.shape[0])
    ]
    for copy in copies:
        copy.start()
    for copy in copies:
        copy.wait()


def packed(keys, values, pos, copies):
    rows = keys.shape[0] + PAD
    return pl.pallas_call(
        pack_kernel,
        out_specs=pl.BlockSpec(memory_space=pl.ANY),
        out_shape=jax.ShapeDtypeStruct((copies, rows, 2 * HD), BF16),
        scratch_shapes=[pltpu.VMEM((rows, 2 * HD), BF16), pltpu.SemaphoreType.DMA((copies,))],
        compiler_params=pltpu.CompilerParams(vmem_limit_bytes=VMEM),
        name="pack",
    )(keys, values, pos)


def attention_kernel(
    query_ref, grad_ref, out_ref, lse_ref, pos_ref, kv_ref, dq_ref, dkv_ref, key, key_t, value, acc
):
    step = pl.program_id(0)
    blocks, rows, _ = kv_ref.shape
    keys = rows - PAD
    tokens = query_ref.shape[0]

    @pl.when(step == 0)
    def _():
        acc[...] = jnp.zeros_like(acc)
        for block in range(blocks):
            here = slice(block * keys, (block + 1) * keys)
            key[here, :] = kv_ref[block, :keys, :HD]
            value[here, :] = kv_ref[block, :keys, HD:]
            key_t[:, here] = jnp.transpose(kv_ref[block, :keys, :HD])

    query_pos = pos_ref[...].astype(F32)
    offsets = lax.broadcasted_iota(jnp.int32, (RUN, tokens), 0).astype(F32)
    for chunk in range(blocks * keys // CHUNK):
        here = slice(chunk * CHUNK, (chunk + 1) * CHUNK)
        visible = []
        for run in range(chunk * CHUNK // RUN, (chunk + 1) * CHUNK // RUN):
            block, row = run // (keys // RUN), keys + run % (keys // RUN)
            start = kv_ref[block, row : row + 1, :1].astype(F32) * RUN
            visible.append(offsets <= query_pos - start)
        visible = jnp.concatenate(visible, axis=0)
        key_part = None
        value_part = None
        for i in range(PAIR):
            cols = slice(i * HD, (i + 1) * HD)
            query = query_ref[:, cols]
            grad = grad_ref[:, cols]
            delta = jnp.sum(
                jnp.transpose(grad.astype(F32) * out_ref[:, cols].astype(F32)),
                axis=0,
                keepdims=True,
            )
            lse = lse_ref[pl.ds(step * PAIR + i, 1), :] * LOG2E
            scores = dot(key[here, :], query, ROWS_ROWS)
            probs = jnp.where(visible, jnp.exp2(scores * (FACTOR * LOG2E) - lse), 0.0)
            dprobs = dot(value[here, :], grad, ROWS_ROWS)
            dscores = (probs * (dprobs - delta)).astype(BF16)
            dv = dot(probs.astype(BF16), grad, COLS_ROWS)
            dk = dot(dscores, query, COLS_ROWS)
            dq = jnp.transpose(dot(key_t[:, here], dscores, COLS_ROWS)) * FACTOR
            if chunk == 0:
                dq_ref[:, cols] = dq
            else:
                dq_ref[:, cols] += dq
            key_part = dk if key_part is None else key_part + dk
            value_part = dv if value_part is None else value_part + dv
        acc[here, :HD] += key_part
        acc[here, HD:] += value_part

    @pl.when(step == pl.num_programs(0) - 1)
    def _():
        for block in range(blocks):
            here = slice(block * keys, (block + 1) * keys)
            dkv_ref[block, :, :HD] = (acc[here, :HD] * FACTOR).astype(BF16)
            dkv_ref[block, :, HD:] = acc[here, HD:].astype(BF16)


def attention(query, grad, out, lse, pos, kv):
    tokens, width = query.shape
    heads = width // HD
    blocks, rows, cols = kv.shape
    keys = rows - PAD
    by_head = pl.BlockSpec((tokens, PAIR * HD), lambda h: (0, h))

    def whole(*shape):
        return pl.BlockSpec(shape, lambda h: (0,) * len(shape))

    return pl.pallas_call(
        attention_kernel,
        grid=(heads // PAIR,),
        in_specs=[
            by_head,
            by_head,
            by_head,
            whole(heads, tokens),
            whole(1, tokens),
            whole(blocks, rows, cols),
        ],
        out_specs=[by_head, whole(blocks, keys, cols)],
        out_shape=[
            jax.ShapeDtypeStruct((tokens, width), F32),
            jax.ShapeDtypeStruct((blocks, keys, cols), BF16),
        ],
        scratch_shapes=[
            pltpu.VMEM((blocks * keys, HD), BF16),
            pltpu.VMEM((HD, blocks * keys), BF16),
            pltpu.VMEM((blocks * keys, HD), BF16),
            pltpu.VMEM((blocks * keys, cols), F32),
        ],
        compiler_params=pltpu.CompilerParams(vmem_limit_bytes=VMEM),
        cost_estimate=pl.CostEstimate(
            flops=10 * blocks * keys * tokens * width,
            bytes_accessed=12 * 2**20,
            transcendentals=blocks * keys * tokens * heads,
        ),
        name="attention",
    )(query, grad, out, lse, pos, kv)


def spread_kernel(place_ref, in_ref, *refs):
    outs, block, turned, in_sems, out_sems = refs[:Y], *refs[Y:]
    outer, tokens, width = block.shape
    rows = outs[0].shape[1]
    core, x, y = place_ref[0], place_ref[1], place_ref[2]
    to_x = jnp.bitwise_xor(x, 1 - core)
    shift = X * Y * rows - width
    loads = []
    stores = []
    for i in range(outer):
        start = pl.multiple_of(i * X * Y * rows + to_x * shift, 128)
        loads.append(
            pltpu.make_async_copy(in_ref.at[:, pl.ds(start, width)], block.at[i], in_sems.at[i])
        )
        for j in range(Y):
            to_y = jnp.bitwise_and(y + j, Y - 1)
            start = pl.multiple_of(to_x * (Y * rows - shift) + to_y * rows, 16)
            stores.append(
                pltpu.make_async_copy(
                    turned.at[i, pl.ds(start, rows)], outs[j].at[i], out_sems.at[i, j]
                )
            )
    for load in loads:
        load.start()
    for i in range(outer):
        loads[i].wait()
        turned[i] = jnp.transpose(block[i])
        for store in stores[i * Y : (i + 1) * Y]:
            store.start()
    for store in stores:
        store.wait()


def spread(inputs, place, outer):
    tokens, width = inputs.shape
    rows = width // (outer * X * Y)
    cols = -(-Y * rows // 128) * 128
    anywhere = pl.BlockSpec(memory_space=pl.ANY)
    return pl.pallas_call(
        spread_kernel,
        in_specs=[pl.BlockSpec(memory_space=pltpu.SMEM), anywhere],
        out_specs=[anywhere] * Y,
        out_shape=[jax.ShapeDtypeStruct((outer, rows, tokens), inputs.dtype)] * Y,
        scratch_shapes=[
            pltpu.VMEM((outer, tokens, cols), inputs.dtype),
            pltpu.VMEM((outer, cols, tokens), inputs.dtype),
            pltpu.SemaphoreType.DMA((outer,)),
            pltpu.SemaphoreType.DMA((outer, Y)),
        ],
        compiler_params=pltpu.CompilerParams(vmem_limit_bytes=VMEM),
        name="spread",
    )(place, inputs)


def pass_along(pieces):
    heads, ctx = lax.axis_size("heads"), lax.axis_size("ctx")
    passed = []
    for i, piece in enumerate(pieces):
        route = []
        for h in range(heads):
            for c in range(ctx):
                x, y = divmod(c, Y)
                to_x = x if h % 2 else 1 - x
                route.append((h * ctx + c, h * ctx + to_x * Y + (y + i) % Y))
        passed.append(lax.ppermute(piece, ("heads", "ctx"), route))
    return passed


def join_kernel(place_ref, *refs):
    blocks, out_ref, sems = refs[: 2 * Y], refs[2 * Y], refs[2 * Y + 1]
    core, x, y = place_ref[0], place_ref[1], place_ref[2]
    ctx_mask = jnp.where(core == 0, CTX_ORDER[0], CTX_ORDER[1])
    dp_mask = jnp.where(core == 0, DP_ORDER[0], DP_ORDER[1])
    copies = []
    for k, block in enumerate(blocks):
        at = core if k < Y else 1 - core
        from_x = jnp.bitwise_xor(x, 1 - at)
        from_y = jnp.bitwise_and(y - k % Y + Y, Y - 1)
        place = jnp.bitwise_xor(from_x * Y + from_y, ctx_mask)
        for i in range(block.shape[0]):
            copies.append(
                pltpu.make_async_copy(
                    block.at[i], out_ref.at[place, jnp.bitwise_xor(i, dp_mask)], sems.at[k, i]
                )
            )
    for copy in copies:
        copy.start()
    for copy in copies:
        copy.wait()


def join(own, other, place):
    outer, rows, tokens = own[0].shape
    anywhere = pl.BlockSpec(memory_space=pl.ANY)
    return pl.pallas_call(
        join_kernel,
        in_specs=[pl.BlockSpec(memory_space=pltpu.SMEM)] + [anywhere] * (2 * Y),
        out_specs=anywhere,
        out_shape=jax.ShapeDtypeStruct((2 * Y, outer, rows, tokens), own[0].dtype),
        scratch_shapes=[pltpu.SemaphoreType.DMA((2 * Y, outer))],
        compiler_params=pltpu.CompilerParams(vmem_limit_bytes=16 * 2**20),
        name="join",
    )(place, *own, *other)


def exchange_ctx(parts):
    heads, ctx = lax.axis_size("heads"), lax.axis_size("ctx")
    groups = [[h * ctx + (i ^ CTX_ORDER[h % 2]) for i in range(ctx)] for h in range(heads)]
    return lax.all_to_all(
        parts, ("heads", "ctx"), 0, 0, axis_index_groups=groups, tiled=True
    )


def exchange_dp(parts):
    heads, dp = lax.axis_size("heads"), lax.axis_size("dp")
    groups = [[(i ^ DP_ORDER[h % 2]) * heads + h for i in range(dp)] for h in range(heads)]
    return lax.all_to_all(parts, ("dp", "heads"), 0, 0, axis_index_groups=groups, tiled=True)


def with_neighbour(block):
    devices = range(lax.axis_size("heads"))
    return lax.ppermute(block, "heads", [(i, i ^ 1) for i in devices])


def shards(inputs, queries, keys, values, outputs, out_grad, lse, positions):
    ctx = lax.axis_size("ctx")
    dp = lax.axis_size("dp")
    index = lax.axis_index("ctx")
    place = jnp.stack([lax.axis_index("heads") % 2, index // Y, index % Y])
    kv = exchange_ctx(packed(keys[0], values[0], positions, ctx))
    pieces = spread(inputs[0], place, dp)
    own = pass_along(pieces)
    kv, _ = lax.optimization_barrier((kv, pieces))
    query_grad, partial = attention(
        queries[0], out_grad[0], outputs[0], jnp.transpose(lse[0]), positions, kv
    )
    partial, own = lax.optimization_barrier((partial, own))
    turned = join(own, [with_neighbour(block) for block in own], place)
    partial, turned = lax.optimization_barrier((exchange_ctx(partial), turned))
    both = jnp.sum(partial.astype(F32), axis=0)
    kv_low = jnp.broadcast_to(both.astype(BF16), (ctx,) + both.shape)
    kv_low = exchange_ctx(kv_low)
    turned = turned.reshape(ctx, -1, turned.shape[-1])
    terms = jnp.einsum("srt,stc->rc", turned, kv_low, preferred_element_type=F32)
    terms, both = lax.optimization_barrier((terms.astype(BF16), both))
    terms = exchange_dp(terms.reshape(dp, -1, 2 * HD))
    weight_grad = jnp.sum(terms.astype(F32), axis=0)
    return (query_grad[None], both[None, :, :HD], both[None, :, HD:], weight_grad)


def solution(mesh):
    return jax.shard_map(
        shards,
        mesh=mesh,
        in_specs=(
            P("dp", "ctx", None),
            P("dp", "ctx", "heads"),
            P("dp", "ctx", "heads"),
            P("dp", "ctx", "heads"),
            P("dp", "ctx", "heads"),
            P("dp", "ctx", "heads"),
            P("dp", "ctx", "heads"),
            P("dp", "ctx"),
        ),
        out_specs=(
            P("dp", "ctx", "heads"),
            P("dp", "ctx", "heads"),
            P("dp", "ctx", "heads"),
            P(("dp", "ctx"), "heads"),
        ),
        check_vma=False,
    )
```

```python
import functools
import math

import jax
import jax.numpy as jnp
from jax import lax
from jax.experimental import pallas as pl
from jax.experimental.pallas import tpu as pltpu
from jax.sharding import PartitionSpec as P

HD = 128
RUN = 128
PAD = 16
PAIR = 2
CHUNK = 1024
VMEM = 60 * 2**20
X = 2
Y = 4
PART_ORDER = (0, 3)
WHOLE_ORDER = (0, 6)
DP_ORDER = (2, 6)
FACTOR = HD ** (-0.5)
LOG2E = math.log2(math.e)
BF16 = jnp.bfloat16
F32 = jnp.float32

ROWS_ROWS = (((1,), (1,)), ((), ()))
COLS_ROWS = (((1,), (0,)), ((), ()))


def dot(a, b, dims):
    return lax.dot_general(a, b, dims, preferred_element_type=F32)


def pack_kernel(key_ref, value_ref, pos_ref, out_ref, block, sems):
    tokens = key_ref.shape[0]
    block[:tokens, :HD] = key_ref[...]
    block[:tokens, HD:] = value_ref[...]
    row = lax.broadcasted_iota(jnp.int32, (PAD, 2 * HD), 0)
    number = jnp.zeros((PAD, 2 * HD), F32)
    for run in range(tokens // RUN):
        first = pos_ref[:, run * RUN : run * RUN + 1].astype(F32) * (1.0 / RUN)
        number = jnp.where(row == run, first, number)
    block[tokens:, :] = number.astype(BF16)
    copies = [
        pltpu.make_async_copy(block, out_ref.at[i], sems.at[i]) for i in range(out_ref.shape[0])
    ]
    for copy in copies:
        copy.start()
    for copy in copies:
        copy.wait()


def packed(keys, values, pos, copies):
    rows = keys.shape[0] + PAD
    return pl.pallas_call(
        pack_kernel,
        out_specs=pl.BlockSpec(memory_space=pl.ANY),
        out_shape=jax.ShapeDtypeStruct((copies, rows, 2 * HD), BF16),
        scratch_shapes=[pltpu.VMEM((rows, 2 * HD), BF16), pltpu.SemaphoreType.DMA((copies,))],
        compiler_params=pltpu.CompilerParams(vmem_limit_bytes=VMEM),
        name="pack",
    )(keys, values, pos)


def delta_kernel(grad_ref, out_ref, query_ref, delta_ref):
    del query_ref
    for head in range(delta_ref.shape[0]):
        cols = slice(head * HD, (head + 1) * HD)
        product = grad_ref[:, cols].astype(F32) * out_ref[:, cols].astype(F32)
        delta_ref[head : head + 1, :] = jnp.sum(jnp.transpose(product), axis=0, keepdims=True)


def deltas(grad, out, query):
    tokens, width = grad.shape
    return pl.pallas_call(
        delta_kernel,
        out_shape=jax.ShapeDtypeStruct((width // HD, tokens), F32),
        compiler_params=pltpu.CompilerParams(vmem_limit_bytes=16 * 2**20),
        name="delta",
    )(grad, out, query)


def attention_kernel(
    query_ref, grad_ref, delta_ref, lse_ref, pos_ref, kv_ref, dq_ref, dkv_ref, key_t, acc
):
    step = pl.program_id(0)
    blocks, rows, _ = kv_ref.shape
    keys = rows - PAD
    tokens = query_ref.shape[0]

    def gathered(chunk, cols):
        count = CHUNK // keys
        return jnp.concatenate(
            [kv_ref[chunk * count + i, :keys, cols] for i in range(count)], axis=0
        )

    @pl.when(step == 0)
    def _():
        acc[...] = jnp.zeros_like(acc)
        for block in range(blocks):
            here = slice(block * keys, (block + 1) * keys)
            key_t[:, here] = jnp.transpose(kv_ref[block, :keys, :HD])

    query_pos = pos_ref[...].astype(F32)
    offsets = lax.broadcasted_iota(jnp.int32, (RUN, tokens), 0).astype(F32)
    for chunk in range(blocks * keys // CHUNK):
        here = slice(chunk * CHUNK, (chunk + 1) * CHUNK)
        visible = []
        for run in range(chunk * CHUNK // RUN, (chunk + 1) * CHUNK // RUN):
            block, row = run // (keys // RUN), keys + run % (keys // RUN)
            start = kv_ref[block, row : row + 1, :1].astype(F32) * RUN
            visible.append(offsets <= query_pos - start)
        visible = jnp.concatenate(visible, axis=0)
        key = gathered(chunk, slice(0, HD))
        value = gathered(chunk, slice(HD, 2 * HD))
        key_part = None
        value_part = None
        for i in range(PAIR):
            cols = slice(i * HD, (i + 1) * HD)
            wide = pl.ds(pl.multiple_of((step * PAIR + i) * HD, HD), HD)
            query = query_ref[:, wide]
            grad = grad_ref[:, wide]
            delta = delta_ref[pl.ds(step * PAIR + i, 1), :]
            lse = lse_ref[pl.ds(step * PAIR + i, 1), :] * LOG2E
            scores = dot(key, query, ROWS_ROWS)
            probs = jnp.where(visible, jnp.exp2(scores * (FACTOR * LOG2E) - lse), 0.0)
            dprobs = dot(value, grad, ROWS_ROWS)
            dscores = (probs * (dprobs - delta)).astype(BF16)
            dv = dot(probs.astype(BF16), grad, COLS_ROWS)
            dk = dot(dscores, query, COLS_ROWS)
            dq = jnp.transpose(dot(key_t[:, here], dscores, COLS_ROWS)) * FACTOR
            if chunk == 0:
                dq_ref[:, cols] = dq
            else:
                dq_ref[:, cols] += dq
            key_part = dk if key_part is None else key_part + dk
            value_part = dv if value_part is None else value_part + dv
        acc[here, :HD] += key_part
        acc[here, HD:] += value_part

    @pl.when(step == pl.num_programs(0) - 1)
    def _():
        for block in range(blocks):
            here = slice(block * keys, (block + 1) * keys)
            dkv_ref[block, :, :HD] = (acc[here, :HD] * FACTOR).astype(BF16)
            dkv_ref[block, :, HD:] = acc[here, HD:].astype(BF16)


def attention(query, grad, delta, lse, pos, kv):
    tokens, width = query.shape
    heads = width // HD
    blocks, rows, cols = kv.shape
    keys = rows - PAD
    by_head = pl.BlockSpec((tokens, PAIR * HD), lambda h: (0, h))

    def whole(*shape):
        return pl.BlockSpec(shape, lambda h: (0,) * len(shape))

    return pl.pallas_call(
        attention_kernel,
        grid=(heads // PAIR,),
        in_specs=[
            pl.BlockSpec(memory_space=pltpu.VMEM),
            pl.BlockSpec(memory_space=pltpu.VMEM),
            whole(heads, tokens),
            whole(heads, tokens),
            whole(1, tokens),
            pl.BlockSpec(memory_space=pltpu.VMEM),
        ],
        out_specs=[by_head, whole(blocks, keys, cols)],
        out_shape=[
            jax.ShapeDtypeStruct((tokens, width), F32),
            jax.ShapeDtypeStruct((blocks, keys, cols), BF16),
        ],
        scratch_shapes=[
            pltpu.VMEM((HD, blocks * keys), BF16),
            pltpu.VMEM((blocks * keys, cols), F32),
        ],
        compiler_params=pltpu.CompilerParams(vmem_limit_bytes=32 * 2**20),
        cost_estimate=pl.CostEstimate(
            flops=10 * blocks * keys * tokens * width,
            bytes_accessed=12 * 2**20,
            transcendentals=blocks * keys * tokens * heads,
        ),
        name="attention",
    )(query, grad, delta, lse, pos, kv)


def spread_kernel(place_ref, in_ref, *refs):
    outs, block, turned, in_sems, out_sems = refs[:Y], *refs[Y:]
    outer, tokens, width = block.shape
    rows = outs[0].shape[1]
    core, x, y = place_ref[0], place_ref[1], place_ref[2]
    to_x = jnp.bitwise_xor(x, 1 - core)
    shift = X * Y * rows - width
    loads = []
    stores = []
    for i in range(outer):
        start = pl.multiple_of(i * X * Y * rows + to_x * shift, 128)
        loads.append(
            pltpu.make_async_copy(in_ref.at[:, pl.ds(start, width)], block.at[i], in_sems.at[i])
        )
        for j in range(Y):
            to_y = jnp.bitwise_and(y + j, Y - 1)
            start = pl.multiple_of(to_x * (Y * rows - shift) + to_y * rows, 16)
            stores.append(
                pltpu.make_async_copy(
                    turned.at[i, pl.ds(start, rows)], outs[j].at[i], out_sems.at[i, j]
                )
            )
    for load in loads:
        load.start()
    for i in range(outer):
        loads[i].wait()
        turned[i] = jnp.transpose(block[i])
        for store in stores[i * Y : (i + 1) * Y]:
            store.start()
    for store in stores:
        store.wait()


def spread(inputs, place, outer):
    tokens, width = inputs.shape
    rows = width // (outer * X * Y)
    cols = -(-Y * rows // 128) * 128
    anywhere = pl.BlockSpec(memory_space=pl.ANY)
    return pl.pallas_call(
        spread_kernel,
        in_specs=[pl.BlockSpec(memory_space=pltpu.SMEM), anywhere],
        out_specs=[anywhere] * Y,
        out_shape=[jax.ShapeDtypeStruct((outer, rows, tokens), inputs.dtype)] * Y,
        scratch_shapes=[
            pltpu.VMEM((outer, tokens, cols), inputs.dtype),
            pltpu.VMEM((outer, cols, tokens), inputs.dtype),
            pltpu.SemaphoreType.DMA((outer,)),
            pltpu.SemaphoreType.DMA((outer, Y)),
        ],
        compiler_params=pltpu.CompilerParams(vmem_limit_bytes=VMEM),
        name="spread",
    )(place, inputs)


def pass_along(pieces):
    heads, ctx = lax.axis_size("heads"), lax.axis_size("ctx")
    passed = []
    for i, piece in enumerate(pieces):
        route = []
        for h in range(heads):
            for c in range(ctx):
                x, y = divmod(c, Y)
                to_x = x if h % 2 else 1 - x
                route.append((h * ctx + c, h * ctx + to_x * Y + (y + i) % Y))
        passed.append(lax.ppermute(piece, ("heads", "ctx"), route))
    return passed


def join_kernel(place_ref, *refs):
    blocks, out_ref = refs[:-1], refs[-1]
    core, x, y = place_ref[0], place_ref[1], place_ref[2]
    ctx_mask = jnp.where(core == 0, WHOLE_ORDER[0], WHOLE_ORDER[1])
    dp_mask = jnp.where(core == 0, DP_ORDER[0], DP_ORDER[1])
    for k, block in enumerate(blocks):
        at = core if k < Y else 1 - core
        from_x = jnp.bitwise_xor(x, 1 - at)
        from_y = jnp.bitwise_and(y - k % Y + Y, Y - 1)
        place = jnp.bitwise_xor(from_x * Y + from_y, ctx_mask)
        for i in range(block.shape[0]):
            out_ref[place, jnp.bitwise_xor(i, dp_mask)] = block[i]


def join(own, other, place):
    outer, rows, tokens = own[0].shape
    return pl.pallas_call(
        join_kernel,
        in_specs=[pl.BlockSpec(memory_space=pltpu.SMEM)]
        + [pl.BlockSpec(memory_space=pltpu.VMEM)] * (2 * Y),
        out_shape=jax.ShapeDtypeStruct((2 * Y, outer, rows, tokens), own[0].dtype),
        compiler_params=pltpu.CompilerParams(vmem_limit_bytes=16 * 2**20),
        name="join",
    )(place, *own, *other)


def exchange_ctx(parts, order):
    heads, ctx = lax.axis_size("heads"), lax.axis_size("ctx")
    groups = [[h * ctx + (i ^ order[h % 2]) for i in range(ctx)] for h in range(heads)]
    return lax.all_to_all(
        parts, ("heads", "ctx"), 0, 0, axis_index_groups=groups, tiled=True
    )


def exchange_dp(parts):
    heads, dp = lax.axis_size("heads"), lax.axis_size("dp")
    groups = [[(i ^ DP_ORDER[h % 2]) * heads + h for i in range(dp)] for h in range(heads)]
    return lax.all_to_all(parts, ("dp", "heads"), 0, 0, axis_index_groups=groups, tiled=True)


def with_neighbour(block):
    devices = range(lax.axis_size("heads"))
    return lax.ppermute(block, "heads", [(i, i ^ 1) for i in devices])


def shards(inputs, queries, keys, values, outputs, out_grad, lse, positions):
    ctx = lax.axis_size("ctx")
    dp = lax.axis_size("dp")
    index = lax.axis_index("ctx")
    place = jnp.stack([lax.axis_index("heads") % 2, index // Y, index % Y])
    kv = exchange_ctx(packed(keys[0], values[0], positions, ctx), PART_ORDER)
    pieces = spread(inputs[0], place, dp)
    own = pass_along(pieces)
    delta, _ = lax.optimization_barrier((deltas(out_grad[0], outputs[0], queries[0]), pieces))
    query_grad, partial = attention(
        queries[0], out_grad[0], delta, jnp.transpose(lse[0]), positions, kv
    )
    partial, own = lax.optimization_barrier((partial, own))
    turned = join(own, [with_neighbour(block) for block in own], place)
    both = jnp.sum(exchange_ctx(partial, PART_ORDER).astype(F32), axis=0)
    both, turned = lax.optimization_barrier((both, turned))
    kv_low = jnp.broadcast_to(both.astype(BF16), (ctx,) + both.shape)
    kv_low = exchange_ctx(kv_low, WHOLE_ORDER)
    turned = turned.reshape(ctx, -1, turned.shape[-1])
    terms = jnp.einsum("srt,stc->rc", turned, kv_low, preferred_element_type=F32)
    terms, both = lax.optimization_barrier((terms.astype(BF16), both))
    terms = exchange_dp(terms.reshape(dp, -1, 2 * HD))
    weight_grad = jnp.sum(terms.astype(F32), axis=0)
    return (query_grad[None], both[None, :, :HD], both[None, :, HD:], weight_grad)


def solution(mesh):
    return jax.shard_map(
        shards,
        mesh=mesh,
        in_specs=(
            P("dp", "ctx", None),
            P("dp", "ctx", "heads"),
            P("dp", "ctx", "heads"),
            P("dp", "ctx", "heads"),
            P("dp", "ctx", "heads"),
            P("dp", "ctx", "heads"),
            P("dp", "ctx", "heads"),
            P("dp", "ctx"),
        ),
        out_specs=(
            P("dp", "ctx", "heads"),
            P("dp", "ctx", "heads"),
            P("dp", "ctx", "heads"),
            P(("dp", "ctx"), "heads"),
        ),
        check_vma=False,
    )
```

```python
import functools
import math

import jax
import jax.numpy as jnp
from jax import lax
from jax.experimental import pallas as pl
from jax.experimental.pallas import tpu as pltpu
from jax.sharding import PartitionSpec as P

HD = 128
RUN = 128
PAD = 16
PAIR = 2
CHUNK = 1024
SLAB = 64
GROUP = 8
VMEM = 60 * 2**20
X = 2
Y = 4
PART_ORDER = (0, 3)
WHOLE_ORDER = (0, 6)
DP_ORDER = (2, 6)
FACTOR = HD ** (-0.5)
LOG2E = math.log2(math.e)
BF16 = jnp.bfloat16
F32 = jnp.float32

ROWS_ROWS = (((1,), (1,)), ((), ()))
COLS_ROWS = (((1,), (0,)), ((), ()))


def dot(a, b, dims):
    return lax.dot_general(a, b, dims, preferred_element_type=F32)


def pack_kernel(key_ref, value_ref, pos_ref, out_ref, block, sems):
    tokens = key_ref.shape[0]
    block[:tokens, :HD] = key_ref[...]
    block[:tokens, HD:] = value_ref[...]
    row = lax.broadcasted_iota(jnp.int32, (PAD, 2 * HD), 0)
    number = jnp.zeros((PAD, 2 * HD), F32)
    for run in range(tokens // RUN):
        first = pos_ref[:, run * RUN : run * RUN + 1].astype(F32) * (1.0 / RUN)
        number = jnp.where(row == run, first, number)
    block[tokens:, :] = number.astype(BF16)
    copies = [
        pltpu.make_async_copy(block, out_ref.at[i], sems.at[i]) for i in range(out_ref.shape[0])
    ]
    for copy in copies:
        copy.start()
    for copy in copies:
        copy.wait()


def packed(keys, values, pos, copies):
    rows = keys.shape[0] + PAD
    return pl.pallas_call(
        pack_kernel,
        out_specs=pl.BlockSpec(memory_space=pl.ANY),
        out_shape=jax.ShapeDtypeStruct((copies, rows, 2 * HD), BF16),
        scratch_shapes=[pltpu.VMEM((rows, 2 * HD), BF16), pltpu.SemaphoreType.DMA((copies,))],
        compiler_params=pltpu.CompilerParams(vmem_limit_bytes=VMEM),
        name="pack",
    )(keys, values, pos)


def delta_kernel(grad_ref, out_ref, query_ref, delta_ref):
    del query_ref
    for head in range(delta_ref.shape[0]):
        cols = slice(head * HD, (head + 1) * HD)
        product = grad_ref[:, cols].astype(F32) * out_ref[:, cols].astype(F32)
        delta_ref[head : head + 1, :] = jnp.sum(jnp.transpose(product), axis=0, keepdims=True)


def deltas(grad, out, query):
    tokens, width = grad.shape
    return pl.pallas_call(
        delta_kernel,
        out_shape=jax.ShapeDtypeStruct((width // HD, tokens), F32),
        compiler_params=pltpu.CompilerParams(vmem_limit_bytes=16 * 2**20),
        name="delta",
    )(grad, out, query)


def attention_kernel(
    query_ref, grad_ref, delta_ref, lse_ref, pos_ref, kv_ref, dq_ref, dkv_ref, key_t, acc
):
    step = pl.program_id(0)
    blocks, rows, _ = kv_ref.shape
    keys = rows - PAD
    tokens = query_ref.shape[0]

    def gathered(chunk, cols):
        count = CHUNK // keys
        return jnp.concatenate(
            [kv_ref[chunk * count + i, :keys, cols] for i in range(count)], axis=0
        )

    @pl.when(step == 0)
    def _():
        acc[...] = jnp.zeros_like(acc)
        for block in range(blocks):
            here = slice(block * keys, (block + 1) * keys)
            key_t[:, here] = jnp.transpose(kv_ref[block, :keys, :HD])

    query_pos = pos_ref[...].astype(F32)
    offsets = lax.broadcasted_iota(jnp.int32, (RUN, tokens), 0).astype(F32)
    for chunk in range(blocks * keys // CHUNK):
        here = slice(chunk * CHUNK, (chunk + 1) * CHUNK)
        visible = []
        for run in range(chunk * CHUNK // RUN, (chunk + 1) * CHUNK // RUN):
            block, row = run // (keys // RUN), keys + run % (keys // RUN)
            start = kv_ref[block, row : row + 1, :1].astype(F32) * RUN
            visible.append(offsets <= query_pos - start)
        visible = jnp.concatenate(visible, axis=0)
        key = gathered(chunk, slice(0, HD))
        value = gathered(chunk, slice(HD, 2 * HD))
        key_part = None
        value_part = None
        for i in range(PAIR):
            cols = slice(i * HD, (i + 1) * HD)
            wide = pl.ds(pl.multiple_of((step * PAIR + i) * HD, HD), HD)
            query = query_ref[:, wide]
            grad = grad_ref[:, wide]
            delta = delta_ref[pl.ds(step * PAIR + i, 1), :]
            lse = lse_ref[pl.ds(step * PAIR + i, 1), :] * LOG2E
            scores = dot(key, query, ROWS_ROWS)
            probs = jnp.where(visible, jnp.exp2(scores * (FACTOR * LOG2E) - lse), 0.0)
            dprobs = dot(value, grad, ROWS_ROWS)
            dscores = (probs * (dprobs - delta)).astype(BF16)
            dv = dot(probs.astype(BF16), grad, COLS_ROWS)
            dk = dot(dscores, query, COLS_ROWS)
            dq = jnp.transpose(dot(key_t[:, here], dscores, COLS_ROWS)) * FACTOR
            if chunk == 0:
                dq_ref[:, cols] = dq
            else:
                dq_ref[:, cols] += dq
            key_part = dk if key_part is None else key_part + dk
            value_part = dv if value_part is None else value_part + dv
        acc[here, :HD] += key_part
        acc[here, HD:] += value_part

    @pl.when(step == pl.num_programs(0) - 1)
    def _():
        for block in range(blocks):
            here = slice(block * keys, (block + 1) * keys)
            dkv_ref[block, :, :HD] = (acc[here, :HD] * FACTOR).astype(BF16)
            dkv_ref[block, :, HD:] = acc[here, HD:].astype(BF16)


def attention(query, grad, delta, lse, pos, kv):
    tokens, width = query.shape
    heads = width // HD
    blocks, rows, cols = kv.shape
    keys = rows - PAD
    by_head = pl.BlockSpec((tokens, PAIR * HD), lambda h: (0, h))

    def whole(*shape):
        return pl.BlockSpec(shape, lambda h: (0,) * len(shape))

    return pl.pallas_call(
        attention_kernel,
        grid=(heads // PAIR,),
        in_specs=[
            pl.BlockSpec(memory_space=pltpu.VMEM),
            pl.BlockSpec(memory_space=pltpu.VMEM),
            whole(heads, tokens),
            whole(heads, tokens),
            whole(1, tokens),
            pl.BlockSpec(memory_space=pltpu.VMEM),
        ],
        out_specs=[by_head, whole(blocks, keys, cols)],
        out_shape=[
            jax.ShapeDtypeStruct((tokens, width), F32),
            jax.ShapeDtypeStruct((blocks, keys, cols), BF16),
        ],
        scratch_shapes=[
            pltpu.VMEM((HD, blocks * keys), BF16),
            pltpu.VMEM((blocks * keys, cols), F32),
        ],
        compiler_params=pltpu.CompilerParams(vmem_limit_bytes=32 * 2**20),
        cost_estimate=pl.CostEstimate(
            flops=10 * blocks * keys * tokens * width,
            bytes_accessed=12 * 2**20,
            transcendentals=blocks * keys * tokens * heads,
        ),
        name="attention",
    )(query, grad, delta, lse, pos, kv)


def spread_kernel(place_ref, in_ref, *refs):
    outs, block, turned, in_sems, out_sems = refs[:Y], *refs[Y:]
    outer, tokens, width = block.shape
    rows = outs[0].shape[1]
    core, x, y = place_ref[0], place_ref[1], place_ref[2]
    to_x = jnp.bitwise_xor(x, 1 - core)
    shift = X * Y * rows - width
    loads = []
    stores = []
    for i in range(outer):
        start = pl.multiple_of(i * X * Y * rows + to_x * shift, 128)
        loads.append(
            pltpu.make_async_copy(in_ref.at[:, pl.ds(start, width)], block.at[i], in_sems.at[i])
        )
        for j in range(Y):
            to_y = jnp.bitwise_and(y + j, Y - 1)
            start = pl.multiple_of(to_x * (Y * rows - shift) + to_y * rows, 16)
            stores.append(
                pltpu.make_async_copy(
                    turned.at[i, pl.ds(start, rows)], outs[j].at[i], out_sems.at[i, j]
                )
            )
    for load in loads:
        load.start()
    for i in range(outer):
        loads[i].wait()
        turned[i] = jnp.transpose(block[i])
        for store in stores[i * Y : (i + 1) * Y]:
            store.start()
    for store in stores:
        store.wait()


def spread(inputs, place, outer):
    tokens, width = inputs.shape
    rows = width // (outer * X * Y)
    cols = -(-Y * rows // 128) * 128
    anywhere = pl.BlockSpec(memory_space=pl.ANY)
    return pl.pallas_call(
        spread_kernel,
        in_specs=[pl.BlockSpec(memory_space=pltpu.SMEM), anywhere],
        out_specs=[anywhere] * Y,
        out_shape=[jax.ShapeDtypeStruct((outer, rows, tokens), inputs.dtype)] * Y,
        scratch_shapes=[
            pltpu.VMEM((outer, tokens, cols), inputs.dtype),
            pltpu.VMEM((outer, cols, tokens), inputs.dtype),
            pltpu.SemaphoreType.DMA((outer,)),
            pltpu.SemaphoreType.DMA((outer, Y)),
        ],
        compiler_params=pltpu.CompilerParams(vmem_limit_bytes=VMEM),
        name="spread",
    )(place, inputs)


def pass_along(pieces):
    heads, ctx = lax.axis_size("heads"), lax.axis_size("ctx")
    passed = []
    for i, piece in enumerate(pieces):
        route = []
        for h in range(heads):
            for c in range(ctx):
                x, y = divmod(c, Y)
                to_x = x if h % 2 else 1 - x
                route.append((h * ctx + c, h * ctx + to_x * Y + (y + i) % Y))
        passed.append(lax.ppermute(piece, ("heads", "ctx"), route))
    return passed


def join_kernel(place_ref, *refs):
    blocks, out_ref = refs[:-1], refs[-1]
    core, x, y = place_ref[0], place_ref[1], place_ref[2]
    ctx_mask = jnp.where(core == 0, WHOLE_ORDER[0], WHOLE_ORDER[1])
    dp_mask = jnp.where(core == 0, DP_ORDER[0], DP_ORDER[1])
    for k, block in enumerate(blocks):
        at = core if k < Y else 1 - core
        from_x = jnp.bitwise_xor(x, 1 - at)
        from_y = jnp.bitwise_and(y - k % Y + Y, Y - 1)
        place = jnp.bitwise_xor(from_x * Y + from_y, ctx_mask)
        for i in range(block.shape[0]):
            out_ref[place, jnp.bitwise_xor(i, dp_mask)] = block[i]


def join(own, other, place):
    outer, rows, tokens = own[0].shape
    return pl.pallas_call(
        join_kernel,
        in_specs=[pl.BlockSpec(memory_space=pltpu.SMEM)]
        + [pl.BlockSpec(memory_space=pltpu.VMEM)] * (2 * Y),
        out_shape=jax.ShapeDtypeStruct((2 * Y, outer, rows, tokens), own[0].dtype),
        compiler_params=pltpu.CompilerParams(vmem_limit_bytes=16 * 2**20),
        name="join",
    )(place, *own, *other)


def finish_kernel(parts_ref, key_ref, value_ref, low_ref):
    for start in range(0, parts_ref.shape[1], SLAB):
        here = slice(start, start + SLAB)
        total = parts_ref[0, here, :].astype(F32)
        for i in range(1, parts_ref.shape[0]):
            total = total + parts_ref[i, here, :].astype(F32)
        key_ref[here, :] = total[:, :HD]
        value_ref[here, :] = total[:, HD:]
        low = total.astype(BF16)
        for i in range(low_ref.shape[0]):
            low_ref[i, here, :] = low


def finish(parts):
    _, tokens, cols = parts.shape
    half = jax.ShapeDtypeStruct((tokens, cols // 2), F32)
    return pl.pallas_call(
        finish_kernel,
        in_specs=[pl.BlockSpec(memory_space=pltpu.VMEM)],
        out_shape=[half, half, jax.ShapeDtypeStruct(parts.shape, BF16)],
        compiler_params=pltpu.CompilerParams(vmem_limit_bytes=16 * 2**20),
        name="finish",
    )(parts)


def project_kernel(turned_ref, low_ref, out_ref):
    outer, rows, cols = out_ref.shape
    for start in range(0, outer, GROUP):
        total = None
        for block in range(turned_ref.shape[0]):
            left = turned_ref[block, start : start + GROUP].reshape(GROUP * rows, -1)
            term = dot(left, low_ref[block], COLS_ROWS)
            total = term if total is None else total + term
        out_ref[start : start + GROUP] = total.astype(BF16).reshape(GROUP, rows, cols)


def project(turned, low):
    _, outer, rows, _ = turned.shape
    return pl.pallas_call(
        project_kernel,
        in_specs=[pl.BlockSpec(memory_space=pltpu.VMEM)] * 2,
        out_shape=jax.ShapeDtypeStruct((outer, rows, low.shape[2]), BF16),
        compiler_params=pltpu.CompilerParams(vmem_limit_bytes=24 * 2**20),
        name="project",
    )(turned, low)


def exchange_ctx(parts, order):
    heads, ctx = lax.axis_size("heads"), lax.axis_size("ctx")
    groups = [[h * ctx + (i ^ order[h % 2]) for i in range(ctx)] for h in range(heads)]
    return lax.all_to_all(
        parts, ("heads", "ctx"), 0, 0, axis_index_groups=groups, tiled=True
    )


def exchange_dp(parts):
    heads, dp = lax.axis_size("heads"), lax.axis_size("dp")
    groups = [[(i ^ DP_ORDER[h % 2]) * heads + h for i in range(dp)] for h in range(heads)]
    return lax.all_to_all(parts, ("dp", "heads"), 0, 0, axis_index_groups=groups, tiled=True)


def with_neighbour(block):
    devices = range(lax.axis_size("heads"))
    return lax.ppermute(block, "heads", [(i, i ^ 1) for i in devices])


def shards(inputs, queries, keys, values, outputs, out_grad, lse, positions):
    ctx = lax.axis_size("ctx")
    dp = lax.axis_size("dp")
    index = lax.axis_index("ctx")
    place = jnp.stack([lax.axis_index("heads") % 2, index // Y, index % Y])
    kv = exchange_ctx(packed(keys[0], values[0], positions, ctx), PART_ORDER)
    pieces = spread(inputs[0], place, dp)
    own = pass_along(pieces)
    delta, _ = lax.optimization_barrier((deltas(out_grad[0], outputs[0], queries[0]), pieces))
    query_grad, partial = attention(
        queries[0], out_grad[0], delta, jnp.transpose(lse[0]), positions, kv
    )
    partial, own = lax.optimization_barrier((partial, own))
    turned = join(own, [with_neighbour(block) for block in own], place)
    key_grad, value_grad, low = finish(exchange_ctx(partial, PART_ORDER))
    low, turned = lax.optimization_barrier((low, turned))
    low = exchange_ctx(low, WHOLE_ORDER)
    terms = exchange_dp(project(turned, low))
    weight_grad = jnp.sum(terms.astype(F32), axis=0)
    return (query_grad[None], key_grad[None], value_grad[None], weight_grad)


def solution(mesh):
    return jax.shard_map(
        shards,
        mesh=mesh,
        in_specs=(
            P("dp", "ctx", None),
            P("dp", "ctx", "heads"),
            P("dp", "ctx", "heads"),
            P("dp", "ctx", "heads"),
            P("dp", "ctx", "heads"),
            P("dp", "ctx", "heads"),
            P("dp", "ctx", "heads"),
            P("dp", "ctx"),
        ),
        out_specs=(
            P("dp", "ctx", "heads"),
            P("dp", "ctx", "heads"),
            P("dp", "ctx", "heads"),
            P(("dp", "ctx"), "heads"),
        ),
        check_vma=False,
    )
```

```python
import functools
import math

import jax
import jax.numpy as jnp
from jax import lax
from jax.experimental import pallas as pl
from jax.experimental.pallas import tpu as pltpu
from jax.sharding import PartitionSpec as P

HD = 128
RUN = 128
PAD = 16
PAIR = 2
CHUNK = 4
SLAB = 128
GROUP = 8
VMEM = 60 * 2**20
X = 2
Y = 4
PART_ORDER = (0, 3)
WHOLE_ORDER = (0, 6)
DP_ORDER = (2, 6)
FACTOR = HD ** (-0.5)
LOG2E = math.log2(math.e)
BF16 = jnp.bfloat16
F32 = jnp.float32

ROWS_ROWS = (((1,), (1,)), ((), ()))
COLS_ROWS = (((1,), (0,)), ((), ()))


def dot(a, b, dims):
    return lax.dot_general(a, b, dims, preferred_element_type=F32)


def pack_kernel(key_ref, value_ref, pos_ref, out_ref, block, sems):
    tokens = key_ref.shape[0]
    block[:tokens, :HD] = key_ref[...]
    block[:tokens, HD:] = value_ref[...]
    row = lax.broadcasted_iota(jnp.int32, (PAD, 2 * HD), 0)
    number = jnp.zeros((PAD, 2 * HD), F32)
    for run in range(tokens // RUN):
        first = pos_ref[:, run * RUN : run * RUN + 1].astype(F32) * (1.0 / RUN)
        number = jnp.where(row == run, first, number)
    block[tokens:, :] = number.astype(BF16)
    copies = [
        pltpu.make_async_copy(block, out_ref.at[i], sems.at[i]) for i in range(out_ref.shape[0])
    ]
    for copy in copies:
        copy.start()
    for copy in copies:
        copy.wait()


def packed(keys, values, pos, copies):
    rows = keys.shape[0] + PAD
    return pl.pallas_call(
        pack_kernel,
        out_specs=pl.BlockSpec(memory_space=pl.ANY),
        out_shape=jax.ShapeDtypeStruct((copies, rows, 2 * HD), BF16),
        scratch_shapes=[pltpu.VMEM((rows, 2 * HD), BF16), pltpu.SemaphoreType.DMA((copies,))],
        compiler_params=pltpu.CompilerParams(vmem_limit_bytes=VMEM),
        name="pack",
    )(keys, values, pos)


def delta_kernel(grad_ref, out_ref, query_ref, delta_ref):
    del query_ref
    for head in range(delta_ref.shape[0]):
        cols = slice(head * HD, (head + 1) * HD)
        product = grad_ref[:, cols].astype(F32) * out_ref[:, cols].astype(F32)
        delta_ref[head : head + 1, :] = jnp.sum(jnp.transpose(product), axis=0, keepdims=True)


def deltas(grad, out, query):
    tokens, width = grad.shape
    return pl.pallas_call(
        delta_kernel,
        out_shape=jax.ShapeDtypeStruct((width // HD, tokens), F32),
        compiler_params=pltpu.CompilerParams(vmem_limit_bytes=16 * 2**20),
        name="delta",
    )(grad, out, query)


def attention_kernel(
    query_ref, grad_ref, delta_ref, lse_ref, pos_ref, kv_ref, dq_ref, dkv_ref, key_t, dq, dkv, *sems
):
    dq_sems, dkv_sems = sems
    blocks, rows, _ = kv_ref.shape
    keys = rows - PAD
    tokens, width = query_ref.shape
    wide = PAIR * HD
    dq_stores = [
        pltpu.make_async_copy(
            dq.at[:, pl.ds(i * wide, wide)], dq_ref.at[:, pl.ds(i * wide, wide)], dq_sems.at[i]
        )
        for i in range(width // wide)
    ]
    dkv_stores = [
        pltpu.make_async_copy(dkv.at[i], dkv_ref.at[i], dkv_sems.at[i]) for i in range(blocks)
    ]
    query_pos = pos_ref[...].astype(F32)
    offsets = lax.broadcasted_iota(jnp.int32, (RUN, tokens), 0).astype(F32)
    for first in range(0, blocks, CHUNK):
        chunk = range(first, first + CHUNK)
        visible = []
        for block in chunk:
            here = slice(block * keys, (block + 1) * keys)
            key_t[:, here] = jnp.transpose(kv_ref[block, :keys, :HD])
            for run in range(keys // RUN):
                start = kv_ref[block, keys + run : keys + run + 1, :1].astype(F32) * RUN
                visible.append(offsets <= query_pos - start)
        visible = jnp.concatenate(visible, axis=0)
        key = jnp.concatenate([kv_ref[block, :keys, :HD] for block in chunk], axis=0)
        value = jnp.concatenate([kv_ref[block, :keys, HD:] for block in chunk], axis=0)
        here = slice(first * keys, (first + CHUNK) * keys)
        key_total = None
        value_total = None
        for head in range(width // HD):
            cols = slice(head * HD, (head + 1) * HD)
            query = query_ref[:, cols]
            grad = grad_ref[:, cols]
            delta = delta_ref[head : head + 1, :]
            lse = lse_ref[head : head + 1, :] * LOG2E
            scores = dot(key, query, ROWS_ROWS)
            probs = jnp.where(visible, jnp.exp2(scores * (FACTOR * LOG2E) - lse), 0.0)
            dprobs = dot(value, grad, ROWS_ROWS)
            dscores = (probs * (dprobs - delta)).astype(BF16)
            dv = dot(probs.astype(BF16), grad, COLS_ROWS)
            dk = dot(dscores, query, COLS_ROWS)
            part = jnp.transpose(dot(key_t[:, here], dscores, COLS_ROWS)) * FACTOR
            if first == 0:
                dq[:, cols] = part
            else:
                dq[:, cols] += part
            if first + CHUNK == blocks and head % PAIR == PAIR - 1:
                dq_stores[head // PAIR].start()
            key_total = dk if key_total is None else key_total + dk
            value_total = dv if value_total is None else value_total + dv
        for i, block in enumerate(chunk):
            part = slice(i * keys, (i + 1) * keys)
            dkv[block, :, :HD] = (key_total[part] * FACTOR).astype(BF16)
            dkv[block, :, HD:] = value_total[part].astype(BF16)
            dkv_stores[block].start()
    for store in dq_stores + dkv_stores:
        store.wait()


def attention(query, grad, delta, lse, pos, kv):
    tokens, width = query.shape
    heads = width // HD
    blocks, rows, cols = kv.shape
    keys = rows - PAD
    return pl.pallas_call(
        attention_kernel,
        in_specs=[pl.BlockSpec(memory_space=pltpu.VMEM)] * 6,
        out_specs=[pl.BlockSpec(memory_space=pl.ANY)] * 2,
        out_shape=[
            jax.ShapeDtypeStruct((tokens, width), F32),
            jax.ShapeDtypeStruct((blocks, keys, cols), BF16),
        ],
        scratch_shapes=[
            pltpu.VMEM((HD, blocks * keys), BF16),
            pltpu.VMEM((tokens, width), F32),
            pltpu.VMEM((blocks, keys, cols), BF16),
            pltpu.SemaphoreType.DMA((heads // PAIR,)),
            pltpu.SemaphoreType.DMA((blocks,)),
        ],
        compiler_params=pltpu.CompilerParams(vmem_limit_bytes=32 * 2**20),
        cost_estimate=pl.CostEstimate(
            flops=10 * blocks * keys * tokens * width,
            bytes_accessed=12 * 2**20,
            transcendentals=blocks * keys * tokens * heads,
        ),
        name="attention",
    )(query, grad, delta, lse, pos, kv)


def spread_kernel(place_ref, in_ref, *refs):
    outs, block, turned, in_sems, out_sems = refs[:Y], *refs[Y:]
    outer, tokens, width = block.shape
    rows = outs[0].shape[1]
    core, x, y = place_ref[0], place_ref[1], place_ref[2]
    to_x = jnp.bitwise_xor(x, 1 - core)
    shift = X * Y * rows - width
    loads = []
    stores = []
    for i in range(outer):
        start = pl.multiple_of(i * X * Y * rows + to_x * shift, 128)
        loads.append(
            pltpu.make_async_copy(in_ref.at[:, pl.ds(start, width)], block.at[i], in_sems.at[i])
        )
        for j in range(Y):
            to_y = jnp.bitwise_and(y + j, Y - 1)
            start = pl.multiple_of(to_x * (Y * rows - shift) + to_y * rows, 16)
            stores.append(
                pltpu.make_async_copy(
                    turned.at[i, pl.ds(start, rows)], outs[j].at[i], out_sems.at[i, j]
                )
            )
    for load in loads:
        load.start()
    for i in range(outer):
        loads[i].wait()
        turned[i] = jnp.transpose(block[i])
        for store in stores[i * Y : (i + 1) * Y]:
            store.start()
    for store in stores:
        store.wait()


def spread(inputs, place, outer):
    tokens, width = inputs.shape
    rows = width // (outer * X * Y)
    cols = -(-Y * rows // 128) * 128
    anywhere = pl.BlockSpec(memory_space=pl.ANY)
    return pl.pallas_call(
        spread_kernel,
        in_specs=[pl.BlockSpec(memory_space=pltpu.SMEM), anywhere],
        out_specs=[anywhere] * Y,
        out_shape=[jax.ShapeDtypeStruct((outer, rows, tokens), inputs.dtype)] * Y,
        scratch_shapes=[
            pltpu.VMEM((outer, tokens, cols), inputs.dtype),
            pltpu.VMEM((outer, cols, tokens), inputs.dtype),
            pltpu.SemaphoreType.DMA((outer,)),
            pltpu.SemaphoreType.DMA((outer, Y)),
        ],
        compiler_params=pltpu.CompilerParams(vmem_limit_bytes=VMEM),
        name="spread",
    )(place, inputs)


def pass_along(pieces):
    heads, ctx = lax.axis_size("heads"), lax.axis_size("ctx")
    passed = []
    for i, piece in enumerate(pieces):
        route = []
        for h in range(heads):
            for c in range(ctx):
                x, y = divmod(c, Y)
                to_x = x if h % 2 else 1 - x
                route.append((h * ctx + c, h * ctx + to_x * Y + (y + i) % Y))
        passed.append(lax.ppermute(piece, ("heads", "ctx"), route))
    return passed


def join_kernel(place_ref, *refs):
    blocks, out_ref = refs[:-1], refs[-1]
    core, x, y = place_ref[0], place_ref[1], place_ref[2]
    ctx_mask = jnp.where(core == 0, WHOLE_ORDER[0], WHOLE_ORDER[1])
    dp_mask = jnp.where(core == 0, DP_ORDER[0], DP_ORDER[1])
    for k, block in enumerate(blocks):
        at = core if k < Y else 1 - core
        from_x = jnp.bitwise_xor(x, 1 - at)
        from_y = jnp.bitwise_and(y - k % Y + Y, Y - 1)
        place = jnp.bitwise_xor(from_x * Y + from_y, ctx_mask)
        for i in range(block.shape[0]):
            out_ref[place, jnp.bitwise_xor(i, dp_mask)] = block[i]


def join(own, other, place):
    outer, rows, tokens = own[0].shape
    return pl.pallas_call(
        join_kernel,
        in_specs=[pl.BlockSpec(memory_space=pltpu.SMEM)]
        + [pl.BlockSpec(memory_space=pltpu.VMEM)] * (2 * Y),
        out_shape=jax.ShapeDtypeStruct((2 * Y, outer, rows, tokens), own[0].dtype),
        compiler_params=pltpu.CompilerParams(vmem_limit_bytes=16 * 2**20),
        name="join",
    )(place, *own, *other)


def finish_kernel(parts_ref, key_ref, value_ref, low_ref, parts, sems):
    slabs = range(0, parts.shape[1], SLAB)
    loads = [
        pltpu.make_async_copy(
            parts_ref.at[:, pl.ds(start, SLAB)], parts.at[:, pl.ds(start, SLAB)], sems.at[i]
        )
        for i, start in enumerate(slabs)
    ]
    for load in loads:
        load.start()
    for load, start in zip(loads, slabs):
        load.wait()
        here = slice(start, start + SLAB)
        total = parts[0, here, :].astype(F32)
        for i in range(1, parts.shape[0]):
            total = total + parts[i, here, :].astype(F32)
        key_ref[here, :] = total[:, :HD]
        value_ref[here, :] = total[:, HD:]
        low = total.astype(BF16)
        for i in range(low_ref.shape[0]):
            low_ref[i, here, :] = low


def finish(parts):
    count, tokens, cols = parts.shape
    half = jax.ShapeDtypeStruct((tokens, cols // 2), F32)
    return pl.pallas_call(
        finish_kernel,
        in_specs=[pl.BlockSpec(memory_space=pl.ANY)],
        out_shape=[half, half, jax.ShapeDtypeStruct(parts.shape, BF16)],
        scratch_shapes=[
            pltpu.VMEM((count, tokens, cols), BF16),
            pltpu.SemaphoreType.DMA((tokens // SLAB,)),
        ],
        compiler_params=pltpu.CompilerParams(vmem_limit_bytes=16 * 2**20),
        name="finish",
    )(parts)


def project_kernel(turned_ref, low_ref, out_ref):
    outer, rows, cols = out_ref.shape
    for start in range(0, outer, GROUP):
        total = None
        for block in range(turned_ref.shape[0]):
            left = turned_ref[block, start : start + GROUP].reshape(GROUP * rows, -1)
            term = dot(left, low_ref[block], COLS_ROWS)
            total = term if total is None else total + term
        out_ref[start : start + GROUP] = total.astype(BF16).reshape(GROUP, rows, cols)


def project(turned, low):
    _, outer, rows, _ = turned.shape
    return pl.pallas_call(
        project_kernel,
        in_specs=[pl.BlockSpec(memory_space=pltpu.VMEM)] * 2,
        out_shape=jax.ShapeDtypeStruct((outer, rows, low.shape[2]), BF16),
        compiler_params=pltpu.CompilerParams(vmem_limit_bytes=24 * 2**20),
        name="project",
    )(turned, low)


def exchange_ctx(parts, order):
    heads, ctx = lax.axis_size("heads"), lax.axis_size("ctx")
    groups = [[h * ctx + (i ^ order[h % 2]) for i in range(ctx)] for h in range(heads)]
    return lax.all_to_all(
        parts, ("heads", "ctx"), 0, 0, axis_index_groups=groups, tiled=True
    )


def exchange_dp(parts):
    heads, dp = lax.axis_size("heads"), lax.axis_size("dp")
    groups = [[(i ^ DP_ORDER[h % 2]) * heads + h for i in range(dp)] for h in range(heads)]
    return lax.all_to_all(parts, ("dp", "heads"), 0, 0, axis_index_groups=groups, tiled=True)


def with_neighbour(block):
    devices = range(lax.axis_size("heads"))
    return lax.ppermute(block, "heads", [(i, i ^ 1) for i in devices])


def shards(inputs, queries, keys, values, outputs, out_grad, lse, positions):
    ctx = lax.axis_size("ctx")
    dp = lax.axis_size("dp")
    index = lax.axis_index("ctx")
    place = jnp.stack([lax.axis_index("heads") % 2, index // Y, index % Y])
    kv = exchange_ctx(packed(keys[0], values[0], positions, ctx), PART_ORDER)
    pieces = spread(inputs[0], place, dp)
    own = pass_along(pieces)
    delta, _ = lax.optimization_barrier((deltas(out_grad[0], outputs[0], queries[0]), pieces))
    query_grad, partial = attention(
        queries[0], out_grad[0], delta, jnp.transpose(lse[0]), positions, kv
    )
    partial, own = lax.optimization_barrier((partial, own))
    turned = join(own, [with_neighbour(block) for block in own], place)
    key_grad, value_grad, low = finish(exchange_ctx(partial, PART_ORDER))
    low, turned = lax.optimization_barrier((low, turned))
    low = exchange_ctx(low, WHOLE_ORDER)
    terms = exchange_dp(project(turned, low))
    weight_grad = jnp.sum(terms.astype(F32), axis=0)
    return (query_grad[None], key_grad[None], value_grad[None], weight_grad)


def solution(mesh):
    return jax.shard_map(
        shards,
        mesh=mesh,
        in_specs=(
            P("dp", "ctx", None),
            P("dp", "ctx", "heads"),
            P("dp", "ctx", "heads"),
            P("dp", "ctx", "heads"),
            P("dp", "ctx", "heads"),
            P("dp", "ctx", "heads"),
            P("dp", "ctx", "heads"),
            P("dp", "ctx"),
        ),
        out_specs=(
            P("dp", "ctx", "heads"),
            P("dp", "ctx", "heads"),
            P("dp", "ctx", "heads"),
            P(("dp", "ctx"), "heads"),
        ),
        check_vma=False,
    )
```

```python
import functools
import math

import jax
import jax.numpy as jnp
from jax import lax
from jax.experimental import pallas as pl
from jax.experimental.pallas import tpu as pltpu
from jax.sharding import PartitionSpec as P

HD = 128
RUN = 128
PAD = 16
PAIR = 2
CHUNK = 4
SLAB = 128
GROUP = 8
VMEM = 60 * 2**20
X = 2
Y = 4
PART_ORDER = (0, 3)
WHOLE_ORDER = (0, 6)
DP_ORDER = (2, 6)
FACTOR = HD ** (-0.5)
LOG2E = math.log2(math.e)
BF16 = jnp.bfloat16
F32 = jnp.float32

ROWS_ROWS = (((1,), (1,)), ((), ()))
COLS_ROWS = (((1,), (0,)), ((), ()))


def dot(a, b, dims):
    return lax.dot_general(a, b, dims, preferred_element_type=F32)


def pack_kernel(key_ref, value_ref, pos_ref, out_ref, block, sems):
    tokens = key_ref.shape[0]
    block[:tokens, :HD] = key_ref[...]
    block[:tokens, HD:] = value_ref[...]
    row = lax.broadcasted_iota(jnp.int32, (PAD, 2 * HD), 0)
    number = jnp.zeros((PAD, 2 * HD), F32)
    for run in range(tokens // RUN):
        first = pos_ref[:, run * RUN : run * RUN + 1].astype(F32) * (1.0 / RUN)
        number = jnp.where(row == run, first, number)
    block[tokens:, :] = number.astype(BF16)
    copies = [
        pltpu.make_async_copy(block, out_ref.at[i], sems.at[i]) for i in range(out_ref.shape[0])
    ]
    for copy in copies:
        copy.start()
    for copy in copies:
        copy.wait()


def packed(keys, values, pos, copies):
    rows = keys.shape[0] + PAD
    return pl.pallas_call(
        pack_kernel,
        out_specs=pl.BlockSpec(memory_space=pl.ANY),
        out_shape=jax.ShapeDtypeStruct((copies, rows, 2 * HD), BF16),
        scratch_shapes=[pltpu.VMEM((rows, 2 * HD), BF16), pltpu.SemaphoreType.DMA((copies,))],
        compiler_params=pltpu.CompilerParams(vmem_limit_bytes=VMEM),
        name="pack",
    )(keys, values, pos)


def delta_kernel(grad_ref, out_ref, query_ref, delta_ref):
    del query_ref
    for head in range(delta_ref.shape[0]):
        cols = slice(head * HD, (head + 1) * HD)
        product = grad_ref[:, cols].astype(F32) * out_ref[:, cols].astype(F32)
        delta_ref[head : head + 1, :] = jnp.sum(jnp.transpose(product), axis=0, keepdims=True)


def deltas(grad, out, query):
    tokens, width = grad.shape
    return pl.pallas_call(
        delta_kernel,
        out_shape=jax.ShapeDtypeStruct((width // HD, tokens), F32),
        compiler_params=pltpu.CompilerParams(vmem_limit_bytes=16 * 2**20),
        name="delta",
    )(grad, out, query)


def attention_kernel(
    query_ref, grad_ref, delta_ref, lse_ref, pos_ref, kv_ref, dq_ref, dkv_ref, key_t, dq, dkv, *sems
):
    dq_sems, dkv_sems = sems
    blocks, rows, _ = kv_ref.shape
    keys = rows - PAD
    tokens, width = query_ref.shape
    wide = PAIR * HD
    dq_stores = [
        pltpu.make_async_copy(
            dq.at[:, pl.ds(i * wide, wide)], dq_ref.at[:, pl.ds(i * wide, wide)], dq_sems.at[i]
        )
        for i in range(width // wide)
    ]
    dkv_stores = [
        pltpu.make_async_copy(dkv.at[i], dkv_ref.at[i], dkv_sems.at[i]) for i in range(blocks)
    ]
    query_pos = pos_ref[...].astype(F32)
    offsets = lax.broadcasted_iota(jnp.int32, (RUN, tokens), 0).astype(F32)
    for first in range(0, blocks, CHUNK):
        chunk = range(first, first + CHUNK)
        visible = []
        for block in chunk:
            here = slice(block * keys, (block + 1) * keys)
            key_t[:, here] = jnp.transpose(kv_ref[block, :keys, :HD])
            for run in range(keys // RUN):
                start = kv_ref[block, keys + run : keys + run + 1, :1].astype(F32) * RUN
                visible.append(offsets <= query_pos - start)
        visible = jnp.concatenate(visible, axis=0)
        key = jnp.concatenate([kv_ref[block, :keys, :HD] for block in chunk], axis=0)
        value = jnp.concatenate([kv_ref[block, :keys, HD:] for block in chunk], axis=0)
        here = slice(first * keys, (first + CHUNK) * keys)
        key_total = None
        value_total = None
        for head in range(width // HD):
            cols = slice(head * HD, (head + 1) * HD)
            query = query_ref[:, cols]
            grad = grad_ref[:, cols]
            delta = delta_ref[head : head + 1, :]
            lse = lse_ref[head : head + 1, :] * LOG2E
            scores = dot(key, query, ROWS_ROWS)
            probs = jnp.where(visible, jnp.exp2(scores * (FACTOR * LOG2E) - lse), 0.0)
            dprobs = dot(value, grad, ROWS_ROWS)
            dscores = (probs * (dprobs - delta)).astype(BF16)
            dv = dot(probs.astype(BF16), grad, COLS_ROWS)
            dk = dot(dscores, query, COLS_ROWS)
            part = jnp.transpose(dot(key_t[:, here], dscores, COLS_ROWS)) * FACTOR
            if first == 0:
                dq[:, cols] = part
            else:
                dq[:, cols] += part
            if first + CHUNK == blocks and head % PAIR == PAIR - 1:
                dq_stores[head // PAIR].start()
            key_total = dk if key_total is None else key_total + dk
            value_total = dv if value_total is None else value_total + dv
        for i, block in enumerate(chunk):
            part = slice(i * keys, (i + 1) * keys)
            dkv[block, :, :HD] = (key_total[part] * FACTOR).astype(BF16)
            dkv[block, :, HD:] = value_total[part].astype(BF16)
            dkv_stores[block].start()
    for store in dq_stores + dkv_stores:
        store.wait()


def attention(query, grad, delta, lse, pos, kv):
    tokens, width = query.shape
    heads = width // HD
    blocks, rows, cols = kv.shape
    keys = rows - PAD
    return pl.pallas_call(
        attention_kernel,
        in_specs=[pl.BlockSpec(memory_space=pltpu.VMEM)] * 6,
        out_specs=[pl.BlockSpec(memory_space=pl.ANY)] * 2,
        out_shape=[
            jax.ShapeDtypeStruct((tokens, width), F32),
            jax.ShapeDtypeStruct((blocks, keys, cols), BF16),
        ],
        scratch_shapes=[
            pltpu.VMEM((HD, blocks * keys), BF16),
            pltpu.VMEM((tokens, width), F32),
            pltpu.VMEM((blocks, keys, cols), BF16),
            pltpu.SemaphoreType.DMA((heads // PAIR,)),
            pltpu.SemaphoreType.DMA((blocks,)),
        ],
        compiler_params=pltpu.CompilerParams(vmem_limit_bytes=32 * 2**20),
        cost_estimate=pl.CostEstimate(
            flops=10 * blocks * keys * tokens * width,
            bytes_accessed=12 * 2**20,
            transcendentals=blocks * keys * tokens * heads,
        ),
        name="attention",
    )(query, grad, delta, lse, pos, kv)


def spread_kernel(place_ref, in_ref, *refs):
    outs, block, turned, in_sems, out_sems = refs[:Y], *refs[Y:]
    outer, tokens, width = block.shape
    rows = outs[0].shape[1]
    core, x, y = place_ref[0], place_ref[1], place_ref[2]
    to_x = jnp.bitwise_xor(x, 1 - core)
    shift = X * Y * rows - width
    loads = []
    stores = []
    for i in range(outer):
        start = pl.multiple_of(i * X * Y * rows + to_x * shift, 128)
        loads.append(
            pltpu.make_async_copy(in_ref.at[:, pl.ds(start, width)], block.at[i], in_sems.at[i])
        )
        for j in range(Y):
            to_y = jnp.bitwise_and(y + j, Y - 1)
            start = pl.multiple_of(to_x * (Y * rows - shift) + to_y * rows, 16)
            stores.append(
                pltpu.make_async_copy(
                    turned.at[i, pl.ds(start, rows)], outs[j].at[i], out_sems.at[i, j]
                )
            )
    for load in loads:
        load.start()
    for i in range(outer):
        loads[i].wait()
        turned[i] = jnp.transpose(block[i])
        for store in stores[i * Y : (i + 1) * Y]:
            store.start()
    for store in stores:
        store.wait()


def spread(inputs, place, outer):
    tokens, width = inputs.shape
    rows = width // (outer * X * Y)
    cols = -(-Y * rows // 128) * 128
    anywhere = pl.BlockSpec(memory_space=pl.ANY)
    return pl.pallas_call(
        spread_kernel,
        in_specs=[pl.BlockSpec(memory_space=pltpu.SMEM), anywhere],
        out_specs=[anywhere] * Y,
        out_shape=[jax.ShapeDtypeStruct((outer, rows, tokens), inputs.dtype)] * Y,
        scratch_shapes=[
            pltpu.VMEM((outer, tokens, cols), inputs.dtype),
            pltpu.VMEM((outer, cols, tokens), inputs.dtype),
            pltpu.SemaphoreType.DMA((outer,)),
            pltpu.SemaphoreType.DMA((outer, Y)),
        ],
        compiler_params=pltpu.CompilerParams(vmem_limit_bytes=VMEM),
        name="spread",
    )(place, inputs)


def pass_along(pieces):
    heads, ctx = lax.axis_size("heads"), lax.axis_size("ctx")
    passed = []
    for i, piece in enumerate(pieces):
        route = []
        for h in range(heads):
            for c in range(ctx):
                x, y = divmod(c, Y)
                to_x = x if h % 2 else 1 - x
                route.append((h * ctx + c, h * ctx + to_x * Y + (y + i) % Y))
        passed.append(lax.ppermute(piece, ("heads", "ctx"), route))
    return passed


def join_kernel(place_ref, *refs):
    blocks, out_ref = refs[:-1], refs[-1]
    core, x, y = place_ref[0], place_ref[1], place_ref[2]
    ctx_mask = jnp.where(core == 0, WHOLE_ORDER[0], WHOLE_ORDER[1])
    dp_mask = jnp.where(core == 0, DP_ORDER[0], DP_ORDER[1])
    for k, block in enumerate(blocks):
        at = core if k < Y else 1 - core
        from_x = jnp.bitwise_xor(x, 1 - at)
        from_y = jnp.bitwise_and(y - k % Y + Y, Y - 1)
        place = jnp.bitwise_xor(from_x * Y + from_y, ctx_mask)
        for i in range(block.shape[0]):
            out_ref[place, jnp.bitwise_xor(i, dp_mask)] = block[i]


def join(own, other, place):
    outer, rows, tokens = own[0].shape
    return pl.pallas_call(
        join_kernel,
        in_specs=[pl.BlockSpec(memory_space=pltpu.SMEM)]
        + [pl.BlockSpec(memory_space=pltpu.VMEM)] * (2 * Y),
        out_shape=jax.ShapeDtypeStruct((2 * Y, outer, rows, tokens), own[0].dtype),
        compiler_params=pltpu.CompilerParams(vmem_limit_bytes=16 * 2**20),
        name="join",
    )(place, *own, *other)


def finish_kernel(parts_ref, key_ref, value_ref, low_ref, parts, sems):
    slabs = range(0, parts.shape[1], SLAB)
    loads = [
        pltpu.make_async_copy(
            parts_ref.at[:, pl.ds(start, SLAB)], parts.at[:, pl.ds(start, SLAB)], sems.at[i]
        )
        for i, start in enumerate(slabs)
    ]
    for load in loads:
        load.start()
    for load, start in zip(loads, slabs):
        load.wait()
        here = slice(start, start + SLAB)
        total = parts[0, here, :].astype(F32)
        for i in range(1, parts.shape[0]):
            total = total + parts[i, here, :].astype(F32)
        key_ref[here, :] = total[:, :HD]
        value_ref[here, :] = total[:, HD:]
        low = total.astype(BF16)
        for i in range(low_ref.shape[0]):
            low_ref[i, here, :] = low


def finish(parts):
    count, tokens, cols = parts.shape
    half = jax.ShapeDtypeStruct((tokens, cols // 2), F32)
    return pl.pallas_call(
        finish_kernel,
        in_specs=[pl.BlockSpec(memory_space=pl.ANY)],
        out_shape=[half, half, jax.ShapeDtypeStruct(parts.shape, BF16)],
        scratch_shapes=[
            pltpu.VMEM((count, tokens, cols), BF16),
            pltpu.SemaphoreType.DMA((tokens // SLAB,)),
        ],
        compiler_params=pltpu.CompilerParams(vmem_limit_bytes=16 * 2**20),
        name="finish",
    )(parts)


def project_kernel(turned_ref, low_ref, out_ref):
    outer, rows, cols = out_ref.shape
    for start in range(0, outer, GROUP):
        total = None
        for block in range(turned_ref.shape[0]):
            left = turned_ref[block, start : start + GROUP].reshape(GROUP * rows, -1)
            term = dot(left, low_ref[block], COLS_ROWS)
            total = term if total is None else total + term
        out_ref[start : start + GROUP] = total.astype(BF16).reshape(GROUP, rows, cols)


def project(turned, low):
    _, outer, rows, _ = turned.shape
    return pl.pallas_call(
        project_kernel,
        in_specs=[pl.BlockSpec(memory_space=pltpu.VMEM)] * 2,
        out_shape=jax.ShapeDtypeStruct((outer, rows, low.shape[2]), BF16),
        compiler_params=pltpu.CompilerParams(vmem_limit_bytes=24 * 2**20),
        name="project",
    )(turned, low)


def exchange_ctx(parts, order):
    heads, ctx = lax.axis_size("heads"), lax.axis_size("ctx")
    groups = [[h * ctx + (i ^ order[h % 2]) for i in range(ctx)] for h in range(heads)]
    return lax.all_to_all(
        parts, ("heads", "ctx"), 0, 0, axis_index_groups=groups, tiled=True
    )


def exchange_dp(parts):
    heads, dp = lax.axis_size("heads"), lax.axis_size("dp")
    groups = [[(i ^ DP_ORDER[h % 2]) * heads + h for i in range(dp)] for h in range(heads)]
    return lax.all_to_all(parts, ("dp", "heads"), 0, 0, axis_index_groups=groups, tiled=True)


def with_neighbour(block):
    devices = range(lax.axis_size("heads"))
    return lax.ppermute(block, "heads", [(i, i ^ 1) for i in devices])


def shards(inputs, queries, keys, values, outputs, out_grad, lse, positions):
    ctx = lax.axis_size("ctx")
    dp = lax.axis_size("dp")
    index = lax.axis_index("ctx")
    place = jnp.stack([lax.axis_index("heads") % 2, index // Y, index % Y])
    kv = exchange_ctx(packed(keys[0], values[0], positions, ctx), PART_ORDER)
    pieces = spread(inputs[0], place, dp)
    own = pass_along(pieces)
    delta, _ = lax.optimization_barrier((deltas(out_grad[0], outputs[0], queries[0]), pieces))
    query_grad, partial = attention(
        queries[0], out_grad[0], delta, jnp.transpose(lse[0]), positions, kv
    )
    partial, *early = lax.optimization_barrier((partial, *own[1:]))
    own = own[:1] + early
    turned = join(own, [with_neighbour(block) for block in own], place)
    key_grad, value_grad, low = finish(exchange_ctx(partial, PART_ORDER))
    low, turned = lax.optimization_barrier((low, turned))
    low = exchange_ctx(low, WHOLE_ORDER)
    terms = exchange_dp(project(turned, low))
    weight_grad = jnp.sum(terms.astype(F32), axis=0)
    return (query_grad[None], key_grad[None], value_grad[None], weight_grad)


def solution(mesh):
    return jax.shard_map(
        shards,
        mesh=mesh,
        in_specs=(
            P("dp", "ctx", None),
            P("dp", "ctx", "heads"),
            P("dp", "ctx", "heads"),
            P("dp", "ctx", "heads"),
            P("dp", "ctx", "heads"),
            P("dp", "ctx", "heads"),
            P("dp", "ctx", "heads"),
            P("dp", "ctx"),
        ),
        out_specs=(
            P("dp", "ctx", "heads"),
            P("dp", "ctx", "heads"),
            P("dp", "ctx", "heads"),
            P(("dp", "ctx"), "heads"),
        ),
        check_vma=False,
    )
```

```python
import functools
import math

import jax
import jax.numpy as jnp
from jax import lax
from jax.experimental import pallas as pl
from jax.experimental.pallas import tpu as pltpu
from jax.sharding import PartitionSpec as P

HD = 128
RUN = 128
PAD = 16
PAIR = 2
CHUNK = 4
SLAB = 128
GROUP = 8
VMEM = 60 * 2**20
X = 2
Y = 4
PART_ORDER = (0, 3)
WHOLE_ORDER = (0, 6)
DP_ORDER = (2, 6)
FACTOR = HD ** (-0.5)
LOG2E = math.log2(math.e)
BF16 = jnp.bfloat16
F32 = jnp.float32

ROWS_ROWS = (((1,), (1,)), ((), ()))
COLS_ROWS = (((1,), (0,)), ((), ()))


def dot(a, b, dims):
    return lax.dot_general(a, b, dims, preferred_element_type=F32)


def pack_kernel(key_ref, value_ref, pos_ref, out_ref, block, sems):
    tokens = key_ref.shape[0]
    block[:tokens, :HD] = key_ref[...]
    block[:tokens, HD:] = value_ref[...]
    row = lax.broadcasted_iota(jnp.int32, (PAD, 2 * HD), 0)
    number = jnp.zeros((PAD, 2 * HD), F32)
    for run in range(tokens // RUN):
        first = pos_ref[:, run * RUN : run * RUN + 1].astype(F32) * (1.0 / RUN)
        number = jnp.where(row == run, first, number)
    block[tokens:, :] = number.astype(BF16)
    copies = [
        pltpu.make_async_copy(block, out_ref.at[i], sems.at[i]) for i in range(out_ref.shape[0])
    ]
    for copy in copies:
        copy.start()
    for copy in copies:
        copy.wait()


def packed(keys, values, pos, copies):
    rows = keys.shape[0] + PAD
    return pl.pallas_call(
        pack_kernel,
        out_specs=pl.BlockSpec(memory_space=pl.ANY),
        out_shape=jax.ShapeDtypeStruct((copies, rows, 2 * HD), BF16),
        scratch_shapes=[pltpu.VMEM((rows, 2 * HD), BF16), pltpu.SemaphoreType.DMA((copies,))],
        compiler_params=pltpu.CompilerParams(vmem_limit_bytes=VMEM),
        name="pack",
    )(keys, values, pos)


def delta_kernel(grad_ref, out_ref, query_ref, delta_ref):
    del query_ref
    for head in range(delta_ref.shape[0]):
        cols = slice(head * HD, (head + 1) * HD)
        product = grad_ref[:, cols].astype(F32) * out_ref[:, cols].astype(F32)
        delta_ref[head : head + 1, :] = jnp.sum(jnp.transpose(product), axis=0, keepdims=True)


def deltas(grad, out, query):
    tokens, width = grad.shape
    return pl.pallas_call(
        delta_kernel,
        out_shape=jax.ShapeDtypeStruct((width // HD, tokens), F32),
        compiler_params=pltpu.CompilerParams(vmem_limit_bytes=16 * 2**20),
        name="delta",
    )(grad, out, query)


def attention_kernel(
    query_ref, grad_ref, delta_ref, lse_ref, pos_ref, kv_ref, dq_ref, dkv_ref, key_t, dq, dkv, *sems
):
    dq_sems, dkv_sems = sems
    blocks, rows, _ = kv_ref.shape
    keys = rows - PAD
    tokens, width = query_ref.shape
    wide = PAIR * HD
    dq_stores = [
        pltpu.make_async_copy(
            dq.at[:, pl.ds(i * wide, wide)], dq_ref.at[:, pl.ds(i * wide, wide)], dq_sems.at[i]
        )
        for i in range(width // wide)
    ]
    dkv_stores = [
        pltpu.make_async_copy(dkv.at[i], dkv_ref.at[i], dkv_sems.at[i]) for i in range(blocks)
    ]
    query_pos = pos_ref[...].astype(F32)
    offsets = lax.broadcasted_iota(jnp.int32, (RUN, tokens), 0).astype(F32)
    for first in range(0, blocks, CHUNK):
        chunk = range(first, first + CHUNK)
        visible = []
        for block in chunk:
            here = slice(block * keys, (block + 1) * keys)
            key_t[:, here] = jnp.transpose(kv_ref[block, :keys, :HD])
            for run in range(keys // RUN):
                start = kv_ref[block, keys + run : keys + run + 1, :1].astype(F32) * RUN
                visible.append(offsets <= query_pos - start)
        visible = jnp.concatenate(visible, axis=0)
        key = jnp.concatenate([kv_ref[block, :keys, :HD] for block in chunk], axis=0)
        value = jnp.concatenate([kv_ref[block, :keys, HD:] for block in chunk], axis=0)
        here = slice(first * keys, (first + CHUNK) * keys)
        key_total = None
        value_total = None
        for head in range(width // HD):
            cols = slice(head * HD, (head + 1) * HD)
            query = query_ref[:, cols]
            grad = grad_ref[:, cols]
            delta = delta_ref[head : head + 1, :]
            lse = lse_ref[head : head + 1, :] * LOG2E
            scores = dot(key, query, ROWS_ROWS)
            probs = jnp.where(visible, jnp.exp2(scores * (FACTOR * LOG2E) - lse), 0.0)
            dprobs = dot(value, grad, ROWS_ROWS)
            dscores = (probs * (dprobs - delta)).astype(BF16)
            dv = dot(probs.astype(BF16), grad, COLS_ROWS)
            dk = dot(dscores, query, COLS_ROWS)
            part = jnp.transpose(dot(key_t[:, here], dscores, COLS_ROWS)) * FACTOR
            if first == 0:
                dq[:, cols] = part
            else:
                dq[:, cols] += part
            if first + CHUNK == blocks and head % PAIR == PAIR - 1:
                dq_stores[head // PAIR].start()
            key_total = dk if key_total is None else key_total + dk
            value_total = dv if value_total is None else value_total + dv
        for i, block in enumerate(chunk):
            part = slice(i * keys, (i + 1) * keys)
            dkv[block, :, :HD] = (key_total[part] * FACTOR).astype(BF16)
            dkv[block, :, HD:] = value_total[part].astype(BF16)
            dkv_stores[block].start()
    for store in dq_stores + dkv_stores:
        store.wait()


def attention(query, grad, delta, lse, pos, kv):
    tokens, width = query.shape
    heads = width // HD
    blocks, rows, cols = kv.shape
    keys = rows - PAD
    return pl.pallas_call(
        attention_kernel,
        in_specs=[pl.BlockSpec(memory_space=pltpu.VMEM)] * 6,
        out_specs=[pl.BlockSpec(memory_space=pl.ANY)] * 2,
        out_shape=[
            jax.ShapeDtypeStruct((tokens, width), F32),
            jax.ShapeDtypeStruct((blocks, keys, cols), BF16),
        ],
        scratch_shapes=[
            pltpu.VMEM((HD, blocks * keys), BF16),
            pltpu.VMEM((tokens, width), F32),
            pltpu.VMEM((blocks, keys, cols), BF16),
            pltpu.SemaphoreType.DMA((heads // PAIR,)),
            pltpu.SemaphoreType.DMA((blocks,)),
        ],
        compiler_params=pltpu.CompilerParams(vmem_limit_bytes=32 * 2**20),
        cost_estimate=pl.CostEstimate(
            flops=10 * blocks * keys * tokens * width,
            bytes_accessed=12 * 2**20,
            transcendentals=blocks * keys * tokens * heads,
        ),
        name="attention",
    )(query, grad, delta, lse, pos, kv)


def position():
    index = lax.axis_index("ctx")
    return jnp.bitwise_and(lax.axis_index("heads"), 1), index // Y, jnp.bitwise_and(index, Y - 1)


def spread_kernel(in_ref, *refs):
    outs, block, turned, in_sems, out_sems = refs[:Y], *refs[Y:]
    outer, tokens, width = block.shape
    rows = outs[0].shape[1]
    core, x, y = position()
    to_x = jnp.bitwise_xor(x, 1 - core)
    shift = X * Y * rows - width
    loads = []
    stores = []
    for i in range(outer):
        start = pl.multiple_of(i * X * Y * rows + to_x * shift, 128)
        loads.append(
            pltpu.make_async_copy(in_ref.at[:, pl.ds(start, width)], block.at[i], in_sems.at[i])
        )
        for j in range(Y):
            to_y = jnp.bitwise_and(y + j, Y - 1)
            start = pl.multiple_of(to_x * (Y * rows - shift) + to_y * rows, 16)
            stores.append(
                pltpu.make_async_copy(
                    turned.at[i, pl.ds(start, rows)], outs[j].at[i], out_sems.at[i, j]
                )
            )
    for load in loads:
        load.start()
    for i in range(outer):
        loads[i].wait()
        turned[i] = jnp.transpose(block[i])
        for store in stores[i * Y : (i + 1) * Y]:
            store.start()
    for store in stores:
        store.wait()


def spread(inputs, outer):
    tokens, width = inputs.shape
    rows = width // (outer * X * Y)
    cols = -(-Y * rows // 128) * 128
    anywhere = pl.BlockSpec(memory_space=pl.ANY)
    return pl.pallas_call(
        spread_kernel,
        in_specs=[anywhere],
        out_specs=[anywhere] * Y,
        out_shape=[jax.ShapeDtypeStruct((outer, rows, tokens), inputs.dtype)] * Y,
        scratch_shapes=[
            pltpu.VMEM((outer, tokens, cols), inputs.dtype),
            pltpu.VMEM((outer, cols, tokens), inputs.dtype),
            pltpu.SemaphoreType.DMA((outer,)),
            pltpu.SemaphoreType.DMA((outer, Y)),
        ],
        compiler_params=pltpu.CompilerParams(vmem_limit_bytes=VMEM),
        name="spread",
    )(inputs)


def pass_along(pieces):
    heads, ctx = lax.axis_size("heads"), lax.axis_size("ctx")
    passed = []
    for i, piece in enumerate(pieces):
        route = []
        for h in range(heads):
            for c in range(ctx):
                x, y = divmod(c, Y)
                to_x = x if h % 2 else 1 - x
                route.append((h * ctx + c, h * ctx + to_x * Y + (y + i) % Y))
        passed.append(lax.ppermute(piece, ("heads", "ctx"), route))
    return passed


def join_kernel(*refs):
    blocks, out_ref = refs[:-1], refs[-1]
    core, x, y = position()
    ctx_mask = jnp.where(core == 0, WHOLE_ORDER[0], WHOLE_ORDER[1])
    dp_mask = jnp.where(core == 0, DP_ORDER[0], DP_ORDER[1])
    for k, block in enumerate(blocks):
        at = core if k < Y else 1 - core
        from_x = jnp.bitwise_xor(x, 1 - at)
        from_y = jnp.bitwise_and(y - k % Y + Y, Y - 1)
        place = jnp.bitwise_xor(from_x * Y + from_y, ctx_mask)
        for i in range(block.shape[0]):
            out_ref[place, jnp.bitwise_xor(i, dp_mask)] = block[i]


def join(own, other):
    outer, rows, tokens = own[0].shape
    return pl.pallas_call(
        join_kernel,
        in_specs=[pl.BlockSpec(memory_space=pltpu.VMEM)] * (2 * Y),
        out_shape=jax.ShapeDtypeStruct((2 * Y, outer, rows, tokens), own[0].dtype),
        compiler_params=pltpu.CompilerParams(vmem_limit_bytes=16 * 2**20),
        name="join",
    )(*own, *other)


def finish_kernel(parts_ref, key_ref, value_ref, low_ref, parts, sems):
    slabs = range(0, parts.shape[1], SLAB)
    loads = [
        pltpu.make_async_copy(
            parts_ref.at[:, pl.ds(start, SLAB)], parts.at[:, pl.ds(start, SLAB)], sems.at[i]
        )
        for i, start in enumerate(slabs)
    ]
    for load in loads:
        load.start()
    for load, start in zip(loads, slabs):
        load.wait()
        here = slice(start, start + SLAB)
        total = parts[0, here, :].astype(F32)
        for i in range(1, parts.shape[0]):
            total = total + parts[i, here, :].astype(F32)
        key_ref[here, :] = total[:, :HD]
        value_ref[here, :] = total[:, HD:]
        low = total.astype(BF16)
        for i in range(low_ref.shape[0]):
            low_ref[i, here, :] = low


def finish(parts):
    count, tokens, cols = parts.shape
    half = jax.ShapeDtypeStruct((tokens, cols // 2), F32)
    return pl.pallas_call(
        finish_kernel,
        in_specs=[pl.BlockSpec(memory_space=pl.ANY)],
        out_shape=[half, half, jax.ShapeDtypeStruct(parts.shape, BF16)],
        scratch_shapes=[
            pltpu.VMEM((count, tokens, cols), BF16),
            pltpu.SemaphoreType.DMA((tokens // SLAB,)),
        ],
        compiler_params=pltpu.CompilerParams(vmem_limit_bytes=16 * 2**20),
        name="finish",
    )(parts)


def project_kernel(turned_ref, low_ref, out_ref):
    outer, rows, cols = out_ref.shape
    for start in range(0, outer, GROUP):
        total = None
        for block in range(turned_ref.shape[0]):
            left = turned_ref[block, start : start + GROUP].reshape(GROUP * rows, -1)
            term = dot(left, low_ref[block], COLS_ROWS)
            total = term if total is None else total + term
        out_ref[start : start + GROUP] = total.astype(BF16).reshape(GROUP, rows, cols)


def project(turned, low):
    _, outer, rows, _ = turned.shape
    return pl.pallas_call(
        project_kernel,
        in_specs=[pl.BlockSpec(memory_space=pltpu.VMEM)] * 2,
        out_shape=jax.ShapeDtypeStruct((outer, rows, low.shape[2]), BF16),
        compiler_params=pltpu.CompilerParams(vmem_limit_bytes=24 * 2**20),
        name="project",
    )(turned, low)


def exchange_ctx(parts, order):
    heads, ctx = lax.axis_size("heads"), lax.axis_size("ctx")
    groups = [[h * ctx + (i ^ order[h % 2]) for i in range(ctx)] for h in range(heads)]
    return lax.all_to_all(
        parts, ("heads", "ctx"), 0, 0, axis_index_groups=groups, tiled=True
    )


def exchange_dp(parts):
    heads, dp = lax.axis_size("heads"), lax.axis_size("dp")
    groups = [[(i ^ DP_ORDER[h % 2]) * heads + h for i in range(dp)] for h in range(heads)]
    return lax.all_to_all(parts, ("dp", "heads"), 0, 0, axis_index_groups=groups, tiled=True)


def with_neighbour(block):
    devices = range(lax.axis_size("heads"))
    return lax.ppermute(block, "heads", [(i, i ^ 1) for i in devices])


def shards(inputs, queries, keys, values, outputs, out_grad, lse, positions):
    ctx = lax.axis_size("ctx")
    dp = lax.axis_size("dp")
    kv = exchange_ctx(packed(keys[0], values[0], positions, ctx), PART_ORDER)
    pieces = spread(inputs[0], dp)
    own = pass_along(pieces)
    delta, _ = lax.optimization_barrier((deltas(out_grad[0], outputs[0], queries[0]), pieces))
    query_grad, partial = attention(
        queries[0], out_grad[0], delta, jnp.transpose(lse[0]), positions, kv
    )
    partial, own = lax.optimization_barrier((partial, own))
    turned = join(own, [with_neighbour(block) for block in own])
    key_grad, value_grad, low = finish(exchange_ctx(partial, PART_ORDER))
    low, turned = lax.optimization_barrier((low, turned))
    low = exchange_ctx(low, WHOLE_ORDER)
    terms = exchange_dp(project(turned, low))
    weight_grad = jnp.sum(terms.astype(F32), axis=0)
    return (query_grad[None], key_grad[None], value_grad[None], weight_grad)


def solution(mesh):
    return jax.shard_map(
        shards,
        mesh=mesh,
        in_specs=(
            P("dp", "ctx", None),
            P("dp", "ctx", "heads"),
            P("dp", "ctx", "heads"),
            P("dp", "ctx", "heads"),
            P("dp", "ctx", "heads"),
            P("dp", "ctx", "heads"),
            P("dp", "ctx", "heads"),
            P("dp", "ctx"),
        ),
        out_specs=(
            P("dp", "ctx", "heads"),
            P("dp", "ctx", "heads"),
            P("dp", "ctx", "heads"),
            P(("dp", "ctx"), "heads"),
        ),
        check_vma=False,
    )
```

```python
import functools
import math

import jax
import jax.numpy as jnp
from jax import lax
from jax.experimental import pallas as pl
from jax.experimental.pallas import tpu as pltpu
from jax.sharding import PartitionSpec as P

HD = 128
RUN = 128
PAD = 16
PAIR = 2
CHUNK = 4
SLAB = 128
LATE = 2
VMEM = 60 * 2**20
X = 2
Y = 4
PART_ORDER = (0, 3)
WHOLE_ORDER = (0, 6)
DP_ORDER = (2, 6)
FACTOR = HD ** (-0.5)
LOG2E = math.log2(math.e)
BF16 = jnp.bfloat16
F32 = jnp.float32

ROWS_ROWS = (((1,), (1,)), ((), ()))
COLS_ROWS = (((1,), (0,)), ((), ()))


def dot(a, b, dims):
    return lax.dot_general(a, b, dims, preferred_element_type=F32)


def pack_kernel(key_ref, value_ref, pos_ref, out_ref, block, sems):
    tokens = key_ref.shape[0]
    block[:tokens, :HD] = key_ref[...]
    block[:tokens, HD:] = value_ref[...]
    row = lax.broadcasted_iota(jnp.int32, (PAD, 2 * HD), 0)
    number = jnp.zeros((PAD, 2 * HD), F32)
    for run in range(tokens // RUN):
        first = pos_ref[:, run * RUN : run * RUN + 1].astype(F32) * (1.0 / RUN)
        number = jnp.where(row == run, first, number)
    block[tokens:, :] = number.astype(BF16)
    copies = [
        pltpu.make_async_copy(block, out_ref.at[i], sems.at[i]) for i in range(out_ref.shape[0])
    ]
    for copy in copies:
        copy.start()
    for copy in copies:
        copy.wait()


def packed(keys, values, pos, copies):
    rows = keys.shape[0] + PAD
    return pl.pallas_call(
        pack_kernel,
        out_specs=pl.BlockSpec(memory_space=pl.ANY),
        out_shape=jax.ShapeDtypeStruct((copies, rows, 2 * HD), BF16),
        scratch_shapes=[pltpu.VMEM((rows, 2 * HD), BF16), pltpu.SemaphoreType.DMA((copies,))],
        compiler_params=pltpu.CompilerParams(vmem_limit_bytes=VMEM),
        name="pack",
    )(keys, values, pos)


def delta_kernel(grad_ref, out_ref, query_ref, delta_ref):
    del query_ref
    for head in range(delta_ref.shape[0]):
        cols = slice(head * HD, (head + 1) * HD)
        product = grad_ref[:, cols].astype(F32) * out_ref[:, cols].astype(F32)
        delta_ref[head : head + 1, :] = jnp.sum(jnp.transpose(product), axis=0, keepdims=True)


def deltas(grad, out, query):
    tokens, width = grad.shape
    return pl.pallas_call(
        delta_kernel,
        out_shape=jax.ShapeDtypeStruct((width // HD, tokens), F32),
        compiler_params=pltpu.CompilerParams(vmem_limit_bytes=16 * 2**20),
        name="delta",
    )(grad, out, query)


def attention_kernel(
    query_ref, grad_ref, delta_ref, lse_ref, pos_ref, kv_ref, dq_ref, dkv_ref, key_t, dq, dkv, *sems
):
    dq_sems, dkv_sems = sems
    blocks, rows, _ = kv_ref.shape
    keys = rows - PAD
    tokens, width = query_ref.shape
    wide = PAIR * HD
    dq_stores = [
        pltpu.make_async_copy(
            dq.at[:, pl.ds(i * wide, wide)], dq_ref.at[:, pl.ds(i * wide, wide)], dq_sems.at[i]
        )
        for i in range(width // wide)
    ]
    dkv_stores = [
        pltpu.make_async_copy(dkv.at[i], dkv_ref.at[i], dkv_sems.at[i]) for i in range(blocks)
    ]
    query_pos = pos_ref[...].astype(F32)
    offsets = lax.broadcasted_iota(jnp.int32, (RUN, tokens), 0).astype(F32)
    for first in range(0, blocks, CHUNK):
        chunk = range(first, first + CHUNK)
        visible = []
        for block in chunk:
            here = slice(block * keys, (block + 1) * keys)
            key_t[:, here] = jnp.transpose(kv_ref[block, :keys, :HD])
            for run in range(keys // RUN):
                start = kv_ref[block, keys + run : keys + run + 1, :1].astype(F32) * RUN
                visible.append(offsets <= query_pos - start)
        visible = jnp.concatenate(visible, axis=0)
        key = jnp.concatenate([kv_ref[block, :keys, :HD] for block in chunk], axis=0)
        value = jnp.concatenate([kv_ref[block, :keys, HD:] for block in chunk], axis=0)
        here = slice(first * keys, (first + CHUNK) * keys)
        key_total = None
        value_total = None
        for head in range(width // HD):
            cols = slice(head * HD, (head + 1) * HD)
            query = query_ref[:, cols]
            grad = grad_ref[:, cols]
            delta = delta_ref[head : head + 1, :]
            lse = lse_ref[head : head + 1, :] * LOG2E
            scores = dot(key, query, ROWS_ROWS)
            probs = jnp.where(visible, jnp.exp2(scores * (FACTOR * LOG2E) - lse), 0.0)
            dprobs = dot(value, grad, ROWS_ROWS)
            dscores = (probs * (dprobs - delta)).astype(BF16)
            dv = dot(probs.astype(BF16), grad, COLS_ROWS)
            dk = dot(dscores, query, COLS_ROWS)
            part = jnp.transpose(dot(key_t[:, here], dscores, COLS_ROWS)) * FACTOR
            if first == 0:
                dq[:, cols] = part
            else:
                dq[:, cols] += part
            if first + CHUNK == blocks and head % PAIR == PAIR - 1:
                dq_stores[head // PAIR].start()
            key_total = dk if key_total is None else key_total + dk
            value_total = dv if value_total is None else value_total + dv
        for i, block in enumerate(chunk):
            part = slice(i * keys, (i + 1) * keys)
            dkv[block, :, :HD] = (key_total[part] * FACTOR).astype(BF16)
            dkv[block, :, HD:] = value_total[part].astype(BF16)
            dkv_stores[block].start()
    for store in dq_stores + dkv_stores:
        store.wait()


def attention(query, grad, delta, lse, pos, kv):
    tokens, width = query.shape
    heads = width // HD
    blocks, rows, cols = kv.shape
    keys = rows - PAD
    return pl.pallas_call(
        attention_kernel,
        in_specs=[pl.BlockSpec(memory_space=pltpu.VMEM)] * 6,
        out_specs=[pl.BlockSpec(memory_space=pl.ANY)] * 2,
        out_shape=[
            jax.ShapeDtypeStruct((tokens, width), F32),
            jax.ShapeDtypeStruct((blocks, keys, cols), BF16),
        ],
        scratch_shapes=[
            pltpu.VMEM((HD, blocks * keys), BF16),
            pltpu.VMEM((tokens, width), F32),
            pltpu.VMEM((blocks, keys, cols), BF16),
            pltpu.SemaphoreType.DMA((heads // PAIR,)),
            pltpu.SemaphoreType.DMA((blocks,)),
        ],
        compiler_params=pltpu.CompilerParams(vmem_limit_bytes=32 * 2**20),
        cost_estimate=pl.CostEstimate(
            flops=10 * blocks * keys * tokens * width,
            bytes_accessed=12 * 2**20,
            transcendentals=blocks * keys * tokens * heads,
        ),
        name="attention",
    )(query, grad, delta, lse, pos, kv)


def position():
    index = lax.axis_index("ctx")
    return jnp.bitwise_and(lax.axis_index("heads"), 1), index // Y, jnp.bitwise_and(index, Y - 1)


def spread_kernel(in_ref, *refs):
    outs, block, turned, in_sems, out_sems = refs[:Y], *refs[Y:]
    outer, tokens, width = block.shape
    rows = outs[0].shape[1]
    core, x, y = position()
    to_x = jnp.bitwise_xor(x, 1 - core)
    shift = X * Y * rows - width
    loads = []
    stores = []
    for i in range(outer):
        start = pl.multiple_of(i * X * Y * rows + to_x * shift, 128)
        loads.append(
            pltpu.make_async_copy(in_ref.at[:, pl.ds(start, width)], block.at[i], in_sems.at[i])
        )
        for j in range(Y):
            to_y = jnp.bitwise_and(y + j, Y - 1)
            start = pl.multiple_of(to_x * (Y * rows - shift) + to_y * rows, 16)
            stores.append(
                pltpu.make_async_copy(
                    turned.at[i, pl.ds(start, rows)], outs[j].at[i], out_sems.at[i, j]
                )
            )
    for load in loads:
        load.start()
    for i in range(outer):
        loads[i].wait()
        turned[i] = jnp.transpose(block[i])
        for store in stores[i * Y : (i + 1) * Y]:
            store.start()
    for store in stores:
        store.wait()


def spread(inputs, outer):
    tokens, width = inputs.shape
    rows = width // (outer * X * Y)
    cols = -(-Y * rows // 128) * 128
    anywhere = pl.BlockSpec(memory_space=pl.ANY)
    return pl.pallas_call(
        spread_kernel,
        in_specs=[anywhere],
        out_specs=[anywhere] * Y,
        out_shape=[jax.ShapeDtypeStruct((outer, rows, tokens), inputs.dtype)] * Y,
        scratch_shapes=[
            pltpu.VMEM((outer, tokens, cols), inputs.dtype),
            pltpu.VMEM((outer, cols, tokens), inputs.dtype),
            pltpu.SemaphoreType.DMA((outer,)),
            pltpu.SemaphoreType.DMA((outer, Y)),
        ],
        compiler_params=pltpu.CompilerParams(vmem_limit_bytes=VMEM),
        name="spread",
    )(inputs)


def pass_along(pieces):
    heads, ctx = lax.axis_size("heads"), lax.axis_size("ctx")
    passed = []
    for i, piece in enumerate(pieces):
        route = []
        for h in range(heads):
            for c in range(ctx):
                x, y = divmod(c, Y)
                to_x = x if h % 2 else 1 - x
                route.append((h * ctx + c, h * ctx + to_x * Y + (y + i) % Y))
        passed.append(lax.ppermute(piece, ("heads", "ctx"), route))
    return passed


def join_kernel(*refs):
    blocks, outs = refs[: 2 * Y], refs[2 * Y :]
    core, x, y = position()
    ctx_mask = jnp.where(core == 0, WHOLE_ORDER[0], WHOLE_ORDER[1])
    dp_mask = jnp.where(core == 0, DP_ORDER[0], DP_ORDER[1])
    for k, block in enumerate(blocks):
        at = core if k < Y else 1 - core
        from_x = jnp.bitwise_xor(x, 1 - at)
        from_y = jnp.bitwise_and(y - k % Y + Y, Y - 1)
        place = jnp.bitwise_xor(from_x * Y + from_y, ctx_mask)
        at = 0
        for out_ref in outs:
            for i in range(out_ref.shape[1]):
                out_ref[place, i] = block[jnp.bitwise_xor(at + i, dp_mask)]
            at += out_ref.shape[1]


def join(own, other):
    outer, rows, tokens = own[0].shape
    return pl.pallas_call(
        join_kernel,
        in_specs=[pl.BlockSpec(memory_space=pltpu.VMEM)] * (2 * Y),
        out_shape=[
            jax.ShapeDtypeStruct((2 * Y, count, rows, tokens), own[0].dtype)
            for count in (outer - LATE, LATE)
        ],
        compiler_params=pltpu.CompilerParams(vmem_limit_bytes=16 * 2**20),
        name="join",
    )(*own, *other)


def finish_kernel(parts_ref, key_ref, value_ref, low_ref, parts, sems):
    slabs = range(0, parts.shape[1], SLAB)
    loads = [
        pltpu.make_async_copy(
            parts_ref.at[:, pl.ds(start, SLAB)], parts.at[:, pl.ds(start, SLAB)], sems.at[i]
        )
        for i, start in enumerate(slabs)
    ]
    for load in loads:
        load.start()
    for load, start in zip(loads, slabs):
        load.wait()
        here = slice(start, start + SLAB)
        total = parts[0, here, :].astype(F32)
        for i in range(1, parts.shape[0]):
            total = total + parts[i, here, :].astype(F32)
        key_ref[here, :] = total[:, :HD]
        value_ref[here, :] = total[:, HD:]
        low = total.astype(BF16)
        for i in range(low_ref.shape[0]):
            low_ref[i, here, :] = low


def finish(parts):
    count, tokens, cols = parts.shape
    half = jax.ShapeDtypeStruct((tokens, cols // 2), F32)
    return pl.pallas_call(
        finish_kernel,
        in_specs=[pl.BlockSpec(memory_space=pl.ANY)],
        out_shape=[half, half, jax.ShapeDtypeStruct(parts.shape, BF16)],
        scratch_shapes=[
            pltpu.VMEM((count, tokens, cols), BF16),
            pltpu.SemaphoreType.DMA((tokens // SLAB,)),
        ],
        compiler_params=pltpu.CompilerParams(vmem_limit_bytes=16 * 2**20),
        name="finish",
    )(parts)


def project_kernel(*refs):
    *turned, low_ref, out_ref = refs
    rows, cols = out_ref.shape[1:]
    at = 0
    for ref in turned:
        blocks, count = ref.shape[:2]
        total = None
        for block in range(blocks):
            left = ref[block].reshape(count * rows, -1)
            term = dot(left, low_ref[block], COLS_ROWS)
            total = term if total is None else total + term
        out_ref[at : at + count] = total.astype(BF16).reshape(count, rows, cols)
        at += count


def project(turned, low):
    rows = turned[0].shape[2]
    outer = sum(part.shape[1] for part in turned)
    return pl.pallas_call(
        project_kernel,
        in_specs=[pl.BlockSpec(memory_space=pltpu.VMEM)] * (len(turned) + 1),
        out_shape=jax.ShapeDtypeStruct((outer, rows, low.shape[2]), BF16),
        compiler_params=pltpu.CompilerParams(vmem_limit_bytes=24 * 2**20),
        name="project",
    )(*turned, low)


def exchange_ctx(parts, order):
    heads, ctx = lax.axis_size("heads"), lax.axis_size("ctx")
    groups = [[h * ctx + (i ^ order[h % 2]) for i in range(ctx)] for h in range(heads)]
    return lax.all_to_all(
        parts, ("heads", "ctx"), 0, 0, axis_index_groups=groups, tiled=True
    )


def exchange_dp(parts):
    heads, dp = lax.axis_size("heads"), lax.axis_size("dp")
    groups = [[(i ^ DP_ORDER[h % 2]) * heads + h for i in range(dp)] for h in range(heads)]
    return lax.all_to_all(parts, ("dp", "heads"), 0, 0, axis_index_groups=groups, tiled=True)


def with_neighbour(block):
    devices = range(lax.axis_size("heads"))
    return lax.ppermute(block, "heads", [(i, i ^ 1) for i in devices])


def shards(inputs, queries, keys, values, outputs, out_grad, lse, positions):
    ctx = lax.axis_size("ctx")
    dp = lax.axis_size("dp")
    kv = exchange_ctx(packed(keys[0], values[0], positions, ctx), PART_ORDER)
    pieces = spread(inputs[0], dp)
    own = pass_along(pieces)
    delta, _ = lax.optimization_barrier((deltas(out_grad[0], outputs[0], queries[0]), pieces))
    query_grad, partial = attention(
        queries[0], out_grad[0], delta, jnp.transpose(lse[0]), positions, kv
    )
    partial, own = lax.optimization_barrier((partial, own))
    turned = join(own, [with_neighbour(block) for block in own])
    key_grad, value_grad, low = finish(exchange_ctx(partial, PART_ORDER))
    low, turned = lax.optimization_barrier((low, turned))
    low = exchange_ctx(low, WHOLE_ORDER)
    terms = exchange_dp(project(turned, low))
    weight_grad = jnp.sum(terms.astype(F32), axis=0)
    return (query_grad[None], key_grad[None], value_grad[None], weight_grad)


def solution(mesh):
    return jax.shard_map(
        shards,
        mesh=mesh,
        in_specs=(
            P("dp", "ctx", None),
            P("dp", "ctx", "heads"),
            P("dp", "ctx", "heads"),
            P("dp", "ctx", "heads"),
            P("dp", "ctx", "heads"),
            P("dp", "ctx", "heads"),
            P("dp", "ctx", "heads"),
            P("dp", "ctx"),
        ),
        out_specs=(
            P("dp", "ctx", "heads"),
            P("dp", "ctx", "heads"),
            P("dp", "ctx", "heads"),
            P(("dp", "ctx"), "heads"),
        ),
        check_vma=False,
    )
```

```python
import functools
import math

import jax
import jax.numpy as jnp
from jax import lax
from jax.experimental import pallas as pl
from jax.experimental.pallas import tpu as pltpu
from jax.sharding import PartitionSpec as P

HD = 128
RUN = 128
PAD = 16
PAIR = 2
CHUNK = 4
SLAB = 128
LATE = 2
VMEM = 60 * 2**20
X = 2
Y = 4
PART_ORDER = (0, 3)
WHOLE_ORDER = (0, 6)
DP_ORDER = (2, 6)
FACTOR = HD ** (-0.5)
LOG2E = math.log2(math.e)
BF16 = jnp.bfloat16
F32 = jnp.float32

ROWS_ROWS = (((1,), (1,)), ((), ()))
COLS_ROWS = (((1,), (0,)), ((), ()))


def dot(a, b, dims):
    return lax.dot_general(a, b, dims, preferred_element_type=F32)


def pack_kernel(key_ref, value_ref, pos_ref, out_ref, block, sems):
    tokens = key_ref.shape[0]
    block[:tokens, :HD] = key_ref[...]
    block[:tokens, HD:] = value_ref[...]
    row = lax.broadcasted_iota(jnp.int32, (PAD, 2 * HD), 0)
    number = jnp.zeros((PAD, 2 * HD), F32)
    for run in range(tokens // RUN):
        first = pos_ref[:, run * RUN : run * RUN + 1].astype(F32) * (1.0 / RUN)
        number = jnp.where(row == run, first, number)
    block[tokens:, :] = number.astype(BF16)
    copies = [
        pltpu.make_async_copy(block, out_ref.at[i], sems.at[i]) for i in range(out_ref.shape[0])
    ]
    for copy in copies:
        copy.start()
    for copy in copies:
        copy.wait()


def packed(keys, values, pos, copies):
    rows = keys.shape[0] + PAD
    return pl.pallas_call(
        pack_kernel,
        out_specs=pl.BlockSpec(memory_space=pl.ANY),
        out_shape=jax.ShapeDtypeStruct((copies, rows, 2 * HD), BF16),
        scratch_shapes=[pltpu.VMEM((rows, 2 * HD), BF16), pltpu.SemaphoreType.DMA((copies,))],
        compiler_params=pltpu.CompilerParams(vmem_limit_bytes=VMEM),
        name="pack",
    )(keys, values, pos)


def delta_kernel(grad_ref, out_ref, query_ref, delta_ref):
    del query_ref
    for head in range(delta_ref.shape[0]):
        cols = slice(head * HD, (head + 1) * HD)
        product = grad_ref[:, cols].astype(F32) * out_ref[:, cols].astype(F32)
        delta_ref[head : head + 1, :] = jnp.sum(jnp.transpose(product), axis=0, keepdims=True)


def deltas(grad, out, query):
    tokens, width = grad.shape
    return pl.pallas_call(
        delta_kernel,
        out_shape=jax.ShapeDtypeStruct((width // HD, tokens), F32),
        compiler_params=pltpu.CompilerParams(vmem_limit_bytes=16 * 2**20),
        name="delta",
    )(grad, out, query)


def attention_kernel(
    query_ref, grad_ref, delta_ref, lse_ref, pos_ref, kv_ref, dq_ref, dkv_ref, key_t, dq, dkv, *sems
):
    dq_sems, dkv_sems = sems
    blocks, rows, _ = kv_ref.shape
    keys = rows - PAD
    tokens, width = query_ref.shape
    wide = PAIR * HD
    dq_stores = [
        pltpu.make_async_copy(
            dq.at[:, pl.ds(i * wide, wide)], dq_ref.at[:, pl.ds(i * wide, wide)], dq_sems.at[i]
        )
        for i in range(width // wide)
    ]
    dkv_stores = [
        pltpu.make_async_copy(dkv.at[i], dkv_ref.at[i], dkv_sems.at[i]) for i in range(blocks)
    ]
    query_pos = pos_ref[...].astype(F32)
    offsets = lax.broadcasted_iota(jnp.int32, (RUN, tokens), 0).astype(F32)
    for first in range(0, blocks, CHUNK):
        chunk = range(first, first + CHUNK)
        visible = []
        for block in chunk:
            here = slice(block * keys, (block + 1) * keys)
            key_t[:, here] = jnp.transpose(kv_ref[block, :keys, :HD])
            for run in range(keys // RUN):
                start = kv_ref[block, keys + run : keys + run + 1, :1].astype(F32) * RUN
                visible.append(offsets <= query_pos - start)
        visible = jnp.concatenate(visible, axis=0)
        key = jnp.concatenate([kv_ref[block, :keys, :HD] for block in chunk], axis=0)
        value = jnp.concatenate([kv_ref[block, :keys, HD:] for block in chunk], axis=0)
        here = slice(first * keys, (first + CHUNK) * keys)
        key_total = None
        value_total = None
        for head in range(width // HD):
            cols = slice(head * HD, (head + 1) * HD)
            query = query_ref[:, cols]
            grad = grad_ref[:, cols]
            delta = delta_ref[head : head + 1, :]
            lse = lse_ref[head : head + 1, :] * LOG2E
            scores = dot(key, query, ROWS_ROWS)
            probs = jnp.where(visible, jnp.exp2(scores * (FACTOR * LOG2E) - lse), 0.0)
            dprobs = dot(value, grad, ROWS_ROWS)
            dscores = (probs * (dprobs - delta)).astype(BF16)
            dv = dot(probs.astype(BF16), grad, COLS_ROWS)
            dk = dot(dscores, query, COLS_ROWS)
            part = jnp.transpose(dot(key_t[:, here], dscores, COLS_ROWS)) * FACTOR
            if first == 0:
                dq[:, cols] = part
            else:
                dq[:, cols] += part
            if first + CHUNK == blocks and head % PAIR == PAIR - 1:
                dq_stores[head // PAIR].start()
            key_total = dk if key_total is None else key_total + dk
            value_total = dv if value_total is None else value_total + dv
        for i, block in enumerate(chunk):
            part = slice(i * keys, (i + 1) * keys)
            dkv[block, :, :HD] = (key_total[part] * FACTOR).astype(BF16)
            dkv[block, :, HD:] = value_total[part].astype(BF16)
            dkv_stores[block].start()
    for store in dq_stores + dkv_stores:
        store.wait()


def attention(query, grad, delta, lse, pos, kv):
    tokens, width = query.shape
    heads = width // HD
    blocks, rows, cols = kv.shape
    keys = rows - PAD
    return pl.pallas_call(
        attention_kernel,
        in_specs=[pl.BlockSpec(memory_space=pltpu.VMEM)] * 6,
        out_specs=[pl.BlockSpec(memory_space=pl.ANY)] * 2,
        out_shape=[
            jax.ShapeDtypeStruct((tokens, width), F32),
            jax.ShapeDtypeStruct((blocks, keys, cols), BF16),
        ],
        scratch_shapes=[
            pltpu.VMEM((HD, blocks * keys), BF16),
            pltpu.VMEM((tokens, width), F32),
            pltpu.VMEM((blocks, keys, cols), BF16),
            pltpu.SemaphoreType.DMA((heads // PAIR,)),
            pltpu.SemaphoreType.DMA((blocks,)),
        ],
        compiler_params=pltpu.CompilerParams(vmem_limit_bytes=32 * 2**20),
        cost_estimate=pl.CostEstimate(
            flops=10 * blocks * keys * tokens * width,
            bytes_accessed=12 * 2**20,
            transcendentals=blocks * keys * tokens * heads,
        ),
        name="attention",
    )(query, grad, delta, lse, pos, kv)


def position():
    index = lax.axis_index("ctx")
    return jnp.bitwise_and(lax.axis_index("heads"), 1), index // Y, jnp.bitwise_and(index, Y - 1)


def spread_kernel(in_ref, *refs):
    outs, block, turned, in_sems, out_sems = refs[:Y], *refs[Y:]
    outer, tokens, width = block.shape
    rows = outs[0].shape[1]
    core, x, y = position()
    to_x = jnp.bitwise_xor(x, 1 - core)
    shift = X * Y * rows - width
    loads = []
    stores = []
    for i in range(outer):
        start = pl.multiple_of(i * X * Y * rows + to_x * shift, 128)
        loads.append(
            pltpu.make_async_copy(in_ref.at[:, pl.ds(start, width)], block.at[i], in_sems.at[i])
        )
        for j in range(Y):
            to_y = jnp.bitwise_and(y + j, Y - 1)
            start = pl.multiple_of(to_x * (Y * rows - shift) + to_y * rows, 16)
            stores.append(
                pltpu.make_async_copy(
                    turned.at[i, pl.ds(start, rows)], outs[j].at[i], out_sems.at[i, j]
                )
            )
    for load in loads:
        load.start()
    for i in range(outer):
        loads[i].wait()
        turned[i] = jnp.transpose(block[i])
        for store in stores[i * Y : (i + 1) * Y]:
            store.start()
    for store in stores:
        store.wait()


def spread(inputs, outer):
    tokens, width = inputs.shape
    rows = width // (outer * X * Y)
    cols = -(-Y * rows // 128) * 128
    anywhere = pl.BlockSpec(memory_space=pl.ANY)
    return pl.pallas_call(
        spread_kernel,
        in_specs=[anywhere],
        out_specs=[anywhere] * Y,
        out_shape=[jax.ShapeDtypeStruct((outer, rows, tokens), inputs.dtype)] * Y,
        scratch_shapes=[
            pltpu.VMEM((outer, tokens, cols), inputs.dtype),
            pltpu.VMEM((outer, cols, tokens), inputs.dtype),
            pltpu.SemaphoreType.DMA((outer,)),
            pltpu.SemaphoreType.DMA((outer, Y)),
        ],
        compiler_params=pltpu.CompilerParams(vmem_limit_bytes=VMEM),
        name="spread",
    )(inputs)


def pass_along(pieces):
    heads, ctx = lax.axis_size("heads"), lax.axis_size("ctx")
    passed = list(pieces)
    for i in (0, 2, 1, 3):
        route = []
        for h in range(heads):
            for c in range(ctx):
                x, y = divmod(c, Y)
                to_x = x if h % 2 else 1 - x
                route.append((h * ctx + c, h * ctx + to_x * Y + (y + i) % Y))
        passed[i] = lax.ppermute(pieces[i], ("heads", "ctx"), route)
    return passed


def join_kernel(*refs):
    blocks, outs = refs[: 2 * Y], refs[2 * Y :]
    core, x, y = position()
    ctx_mask = jnp.where(core == 0, WHOLE_ORDER[0], WHOLE_ORDER[1])
    dp_mask = jnp.where(core == 0, DP_ORDER[0], DP_ORDER[1])
    for k, block in enumerate(blocks):
        at = core if k < Y else 1 - core
        from_x = jnp.bitwise_xor(x, 1 - at)
        from_y = jnp.bitwise_and(y - k % Y + Y, Y - 1)
        place = jnp.bitwise_xor(from_x * Y + from_y, ctx_mask)
        at = 0
        for out_ref in outs:
            for i in range(out_ref.shape[1]):
                out_ref[place, i] = block[jnp.bitwise_xor(at + i, dp_mask)]
            at += out_ref.shape[1]


def join(own, other):
    outer, rows, tokens = own[0].shape
    return pl.pallas_call(
        join_kernel,
        in_specs=[pl.BlockSpec(memory_space=pltpu.VMEM)] * (2 * Y),
        out_shape=[
            jax.ShapeDtypeStruct((2 * Y, count, rows, tokens), own[0].dtype)
            for count in (outer - LATE, LATE)
        ],
        compiler_params=pltpu.CompilerParams(vmem_limit_bytes=16 * 2**20),
        name="join",
    )(*own, *other)


def finish_kernel(parts_ref, key_ref, value_ref, low_ref, parts, sems):
    slabs = range(0, parts.shape[1], SLAB)
    loads = [
        pltpu.make_async_copy(
            parts_ref.at[:, pl.ds(start, SLAB)], parts.at[:, pl.ds(start, SLAB)], sems.at[i]
        )
        for i, start in enumerate(slabs)
    ]
    for load in loads:
        load.start()
    for load, start in zip(loads, slabs):
        load.wait()
        here = slice(start, start + SLAB)
        total = parts[0, here, :].astype(F32)
        for i in range(1, parts.shape[0]):
            total = total + parts[i, here, :].astype(F32)
        key_ref[here, :] = total[:, :HD]
        value_ref[here, :] = total[:, HD:]
        low = total.astype(BF16)
        for i in range(low_ref.shape[0]):
            low_ref[i, here, :] = low


def finish(parts):
    count, tokens, cols = parts.shape
    half = jax.ShapeDtypeStruct((tokens, cols // 2), F32)
    return pl.pallas_call(
        finish_kernel,
        in_specs=[pl.BlockSpec(memory_space=pl.ANY)],
        out_shape=[half, half, jax.ShapeDtypeStruct(parts.shape, BF16)],
        scratch_shapes=[
            pltpu.VMEM((count, tokens, cols), BF16),
            pltpu.SemaphoreType.DMA((tokens // SLAB,)),
        ],
        compiler_params=pltpu.CompilerParams(vmem_limit_bytes=16 * 2**20),
        name="finish",
    )(parts)


def project_kernel(*refs):
    *turned, low_ref, out_ref = refs
    rows, cols = out_ref.shape[1:]
    at = 0
    for ref in turned:
        blocks, count = ref.shape[:2]
        total = None
        for block in range(blocks):
            left = ref[block].reshape(count * rows, -1)
            term = dot(left, low_ref[block], COLS_ROWS)
            total = term if total is None else total + term
        out_ref[at : at + count] = total.astype(BF16).reshape(count, rows, cols)
        at += count


def project(turned, low):
    rows = turned[0].shape[2]
    outer = sum(part.shape[1] for part in turned)
    return pl.pallas_call(
        project_kernel,
        in_specs=[pl.BlockSpec(memory_space=pltpu.VMEM)] * (len(turned) + 1),
        out_shape=jax.ShapeDtypeStruct((outer, rows, low.shape[2]), BF16),
        compiler_params=pltpu.CompilerParams(vmem_limit_bytes=24 * 2**20),
        name="project",
    )(*turned, low)


def exchange_ctx(parts, order):
    heads, ctx = lax.axis_size("heads"), lax.axis_size("ctx")
    groups = [[h * ctx + (i ^ order[h % 2]) for i in range(ctx)] for h in range(heads)]
    return lax.all_to_all(
        parts, ("heads", "ctx"), 0, 0, axis_index_groups=groups, tiled=True
    )


def exchange_dp(parts):
    heads, dp = lax.axis_size("heads"), lax.axis_size("dp")
    groups = [[(i ^ DP_ORDER[h % 2]) * heads + h for i in range(dp)] for h in range(heads)]
    return lax.all_to_all(parts, ("dp", "heads"), 0, 0, axis_index_groups=groups, tiled=True)


def with_neighbour(block):
    devices = range(lax.axis_size("heads"))
    return lax.ppermute(block, "heads", [(i, i ^ 1) for i in devices])


def shards(inputs, queries, keys, values, outputs, out_grad, lse, positions):
    ctx = lax.axis_size("ctx")
    dp = lax.axis_size("dp")
    kv = exchange_ctx(packed(keys[0], values[0], positions, ctx), PART_ORDER)
    pieces = spread(inputs[0], dp)
    own = pass_along(pieces)
    delta, _ = lax.optimization_barrier((deltas(out_grad[0], outputs[0], queries[0]), pieces))
    query_grad, partial = attention(
        queries[0], out_grad[0], delta, jnp.transpose(lse[0]), positions, kv
    )
    own = [own[i] for i in (0, 2, 1, 3)]
    partial, own = lax.optimization_barrier((partial, own))
    own = [own[i] for i in (0, 2, 1, 3)]
    turned = join(own, [with_neighbour(block) for block in own])
    key_grad, value_grad, low = finish(exchange_ctx(partial, PART_ORDER))
    low, turned = lax.optimization_barrier((low, turned))
    low = exchange_ctx(low, WHOLE_ORDER)
    terms = exchange_dp(project(turned, low))
    weight_grad = jnp.sum(terms.astype(F32), axis=0)
    return (query_grad[None], key_grad[None], value_grad[None], weight_grad)


def solution(mesh):
    return jax.shard_map(
        shards,
        mesh=mesh,
        in_specs=(
            P("dp", "ctx", None),
            P("dp", "ctx", "heads"),
            P("dp", "ctx", "heads"),
            P("dp", "ctx", "heads"),
            P("dp", "ctx", "heads"),
            P("dp", "ctx", "heads"),
            P("dp", "ctx", "heads"),
            P("dp", "ctx"),
        ),
        out_specs=(
            P("dp", "ctx", "heads"),
            P("dp", "ctx", "heads"),
            P("dp", "ctx", "heads"),
            P(("dp", "ctx"), "heads"),
        ),
        check_vma=False,
    )
```
